256 devices in a mesh: row: 32 (over y, z), col: 8 (over x, core).
Axes of the slice: x: 4, y: 4, z: 8, core: 2. Of those that a mesh axis runs over, the one named last changes fastest.
Arguments:
- near_tiles: bfloat16 [64, 2, 8, 512, 512], P('row', None, 'col'), may hold values from -3 to 3
- basis_u: bfloat16 [64, 2, 8, 64, 512], P('row', None, 'col'), may hold values from -1.75 to 1.75
- basis_v: bfloat16 [64, 2, 8, 64, 512], P('row', None, 'col'), may hold values from -1.75 to 1.75
- near_mask: int32 [64, 2, 8], P('row', None, 'col'), may hold values from 0 to 1, as said below
- ranks: int32 [64, 2, 8], P('row', None, 'col'), may hold values from 1 to 64
- row_map: int32 [64], replicated, may hold values from 0 to 63, as said below
Outputs:
- factored: bfloat16 [64, 2, 8, 512, 512], P('row', None, 'col')
The draws below stay inside these ranges and needn't reach their ends.
Inputs may be any that keep to these rules, and one draw needn't show every extreme that they name: row_map is a permutation of 0 to 63. near_mask is 1 on every tile whose tile row and tile column differ by at most one.
All inputs are finite; a program needn't handle non-finite values.
Results may differ from the reference program's by a relative error of at most 0.0045.
Values may be sent and summed in bfloat16 or wider, within the bound.
No kernel may reach another device: no remote copies, remote signals or barrier semaphores. Data moves between devices by JAX's collectives and lax.ppermute only.
A program may use at most 64 MiB of HBM per device.

```python
import math
import jax
import jax.numpy as jnp
from jax import lax

TILE = 512
KMAX = 64
NS_STEPS = 3
PANELS = 2
TC = 2
NR = 64
NC = 16
N_COL = 8


def shared_rows(key):
    return jax.random.permutation(jax.random.fold_in(key, 11), NR).astype(jnp.int32)


def tile_gaps(held_rows):
    columns = jnp.arange(NC, dtype=jnp.int32)
    return (jnp.abs(held_rows[:, None] - columns[None, :]), jnp.maximum(held_rows[:, None], columns[None, :]))


def draw_row_map(key, part):
    return shared_rows(key)


def draw_near_mask(key, part):
    held_rows = shared_rows(key)
    key = jax.random.fold_in(key, 23)
    coins = jax.random.randint(key, (NR, NC), 0, 4)
    nearby = (coins == 0).astype(jnp.int32)
    gaps, larger = tile_gaps(held_rows)
    banded = (gaps <= 1).astype(jnp.int32)
    return jnp.maximum(nearby, banded).reshape(NR, TC, N_COL)


def draw_ranks(key, part):
    key = jax.random.fold_in(key, 37)
    values = jax.random.randint(key, (NR, NC), 1, KMAX + 1).astype(jnp.int32)
    values = values.at[0, 0].set(KMAX)
    return values.reshape(NR, TC, N_COL)


def draw_near_tiles(key, part):
    held_rows = shared_rows(key)
    key = jax.random.fold_in(key, 41)
    gaps, larger = tile_gaps(held_rows)
    spread = jnp.where(gaps == 1, jnp.where(larger < PANELS, 0.45, 1.2), 0.25).astype(jnp.float32)
    spread = spread.reshape(NR, TC, N_COL, 1, 1)
    base = jnp.clip(jax.random.normal(key, (NR, TC, N_COL, TILE, TILE), jnp.float32), -2.5, 2.5)
    return (base * spread).astype(jnp.bfloat16)


def level_of(rng, shape, split, low, largest):
    def one(axis_at, parts):
        draws = jax.random.uniform(jax.random.fold_in(jax.random.fold_in(rng, 6), axis_at), (parts,), jnp.float32, low / len(split), largest / len(split))
        return jnp.repeat(jnp.exp(draws), shape[axis_at] // parts).reshape((-1,) + (1,) * (len(shape) - axis_at - 1))

    gain = one(*split[0])
    for cut in split[1:]:
        gain = gain * one(*cut)
    return gain


def bell_draw(stream_key, dims, scale, bound, pieces=(), held_as=jnp.bfloat16):
    values = scale * jax.random.normal(stream_key, dims, jnp.float32)
    if pieces:
        values = values * level_of(stream_key, dims, pieces, -0.22, 0.18)
    return jnp.clip(values, -bound, bound).astype(held_as)


def setup_inputs(seed: int = 0) -> dict:
    streams_of = jax.random.split(jax.random.key(seed), 7)
    near_tiles = draw_near_tiles(jax.random.fold_in(streams_of[6], 71), 0)
    basis_u = bell_draw(streams_of[1], (NR, TC, N_COL, KMAX, TILE), 0.12, 1.75, ((0, 32), (2, 8)))
    basis_v = bell_draw(streams_of[2], (NR, TC, N_COL, KMAX, TILE), 0.12, 1.75, ((0, 32), (2, 8)))
    near_mask = draw_near_mask(jax.random.fold_in(streams_of[6], 71), 0)
    ranks = draw_ranks(jax.random.fold_in(streams_of[6], 71), 0)
    row_map = draw_row_map(jax.random.fold_in(streams_of[6], 71), 0)
    return {"near_tiles": near_tiles, "basis_u": basis_u, "basis_v": basis_v, "near_mask": near_mask, "ranks": ranks, "row_map": row_map}


shift_factor = 1.1

def rounded(values):
    return lax.optimization_barrier(values.astype(jnp.bfloat16)).astype(jnp.float32)

def newton_inverse(pivot_tile):
    identity = jnp.eye(TILE, dtype=jnp.float32)
    approx = identity / (shift_factor * math.sqrt(TILE))
    for sweep in range(NS_STEPS):
        product = jnp.dot(pivot_tile, approx, precision=lax.Precision.HIGHEST)
        approx = jnp.dot(approx, 2.0 * identity - product, precision=lax.Precision.HIGHEST)
    return approx

def reference(near_tiles, basis_u, basis_v, near_mask, ranks, row_map):
    diag_shift = shift_factor * math.sqrt(TILE)
    identity = jnp.eye(TILE, dtype=jnp.float32)
    near_full = near_tiles.reshape(NR, NC, TILE, TILE)
    near_flags = near_mask.reshape(NR, NC)
    rank_rows = ranks.reshape(NR, NC)
    left_basis = basis_u.reshape(NR, NC, KMAX, TILE)
    right_basis = basis_v.reshape(NR, NC, KMAX, TILE)
    on_diag = (row_map[:, None] == jnp.arange(NC, dtype=jnp.int32)[None, :]).astype(jnp.float32)

    def build_row(item):
        near_row, flag_row, rank_row, left_row, right_row, diag_row = item
        kept_cols = (jnp.arange(KMAX, dtype=jnp.int32)[None, :] < rank_row[:, None]).astype(jnp.float32)
        left_kept = left_row.astype(jnp.float32) * kept_cols[:, :, None]
        lowrank = jnp.einsum('jkp,jkq->jpq', left_kept, right_row.astype(jnp.float32))
        dense = jnp.where(flag_row[:, None, None] > 0, near_row.astype(jnp.float32), 0.0)
        return dense + lowrank + diag_shift * diag_row[:, None, None] * identity
    matrix = lax.map(build_row, (near_full, near_flags, rank_rows, left_basis, right_basis, on_diag))
    for elimination in range(PANELS):
        owner_slot = jnp.sum(jnp.where(row_map == elimination, jnp.arange(NR, dtype=jnp.int32), 0)).astype(jnp.int32)
        pivot_tile = matrix[owner_slot, elimination]
        inverse = rounded(newton_inverse(pivot_tile))
        column_tiles = rounded(matrix[:, elimination])
        multipliers = rounded(jnp.einsum('spq,qr->spr', column_tiles, inverse))
        row_tiles = rounded(matrix[owner_slot])
        col_live = jnp.arange(NC, dtype=jnp.int32) > elimination
        row_live = row_map > elimination

        def apply_row(item):
            row_block, mult_row, alive = item
            change = jnp.einsum('pq,jqr->jpr', mult_row, row_tiles)
            return row_block - jnp.where((alive & col_live)[:, None, None], change, 0.0)
        matrix = lax.map(apply_row, (matrix, multipliers, row_live))
    return matrix.astype(jnp.bfloat16).reshape(NR, TC, N_COL, TILE, TILE)
```

```python
import math

import jax
import jax.numpy as jnp
from jax import lax
from jax.sharding import PartitionSpec as P

TILE = 512
KMAX = 64
RAW = TILE + 2 * KMAX
LANES = 128
BLOCKS = TILE // LANES
SHIFT = 1.1 * math.sqrt(TILE)
NY, NZ, NX = 4, 8, 4
BF = jnp.bfloat16
F32 = jnp.float32


def dot(a, b):
    return jnp.dot(a, b, preferred_element_type=F32)


def dot_hi(a, b):
    return jnp.dot(a, b, precision=lax.Precision.HIGHEST)


def pack(raw):
    lead = raw.shape[:-2]
    raw = raw.reshape(*lead, RAW, BLOCKS, LANES)
    return jnp.swapaxes(raw, -3, -2).reshape(*lead, BLOCKS * RAW, LANES)


def unpack(packed):
    lead = packed.shape[:-2]
    packed = packed.reshape(*lead, BLOCKS, RAW, LANES)
    return jnp.swapaxes(packed, -3, -2).reshape(*lead, RAW, TILE)


def build(raw, diag):
    near = raw[:TILE].astype(F32)
    left, right = raw[TILE : TILE + KMAX], raw[TILE + KMAX :]
    low = lax.dot_general(left, right, (((0,), (0,)), ((), ())), preferred_element_type=F32)
    return near + low + jnp.where(diag, SHIFT, 0.0) * jnp.eye(TILE, dtype=F32)


def inverse(pivot):
    eye = jnp.eye(TILE, dtype=F32)
    e = eye - pivot * (1.0 / SHIFT)
    e2 = dot_hi(e, e)
    s = eye + e + e2 + dot_hi(e, e2)
    e4 = dot_hi(e2, e2)
    return ((s + dot_hi(s, e4)) * (1.0 / SHIFT)).astype(BF)


def col_pairs(dx):
    return [(core, dx * 2 + core) for core in range(2)]


def spread_x(value, x):
    parts = [lax.ppermute(value, "col", col_pairs(dx)) for dx in (1, 3, 2)]
    return jnp.where(x == 0, value, parts[0] + parts[1] + parts[2])


def swap_cores(value, core):
    other = lax.ppermute(value, "col", [(c, c ^ 1) for c in range(2 * NX)])
    return jnp.where(core == 0, value, other), jnp.where(core == 0, other, value)


def body(near_tiles, basis_u, basis_v, near_mask, ranks, row_map):
    row = lax.axis_index("row")
    col = lax.axis_index("col")
    x, core = col // 2, col % 2
    near = near_tiles.reshape(2, 2, TILE, TILE)
    kept = jnp.arange(KMAX, dtype=jnp.int32)[None, None, :] < ranks.reshape(2, 2)[:, :, None]
    left = jnp.where(kept[..., None], basis_u.reshape(2, 2, KMAX, TILE), 0)
    near = jnp.where(near_mask.reshape(2, 2, 1, 1) > 0, near, 0)
    raw = jnp.concatenate([near, left, basis_v.reshape(2, 2, KMAX, TILE)], axis=2)
    slots = jnp.arange(64, dtype=jnp.int32)
    owner = [jnp.sum(jnp.where(row_map == k, slots, 0)) for k in range(2)]
    owner_row = [o // 2 for o in owner]
    held = lax.dynamic_slice_in_dim(row_map, row * 2, 2)

    cols = spread_x(raw[:, 0], x)
    cols = swap_cores(cols, core)

    def payload(slot):
        tiles = lax.dynamic_index_in_dim(raw, slot, 0, keepdims=False)
        return jnp.swapaxes(pack(tiles).reshape(2, 32, -1, LANES), 0, 1)

    def scatter(slot):
        return lax.all_to_all(payload(slot), "row", 0, 0)

    def take(got, k):
        return lax.dynamic_index_in_dim(got, owner_row[k], 0, keepdims=False)

    def apart():
        return jnp.stack([take(scatter(owner[k] % 2), k) for k in range(2)])

    def merged():
        slot = jnp.where(row == owner_row[0], owner[0], owner[1]) % 2
        got = scatter(slot)
        return jnp.stack([take(got, k) for k in range(2)])

    chunk = lax.cond(owner_row[0] == owner_row[1], apart, merged)
    pivots = spread_x(chunk[:, 0], x)
    bundle = jnp.concatenate([pivots, chunk.reshape(4, -1, LANES)])
    z_groups = [[y * NZ + z for z in range(NZ)] for y in range(NY)]
    y_groups = [[y * NZ + z for y in range(NY)] for z in range(NZ)]

    def gather(value, count, groups):
        return lax.all_to_all(
            jnp.broadcast_to(value[None], (count, *value.shape)), "row", 0, 0, axis_index_groups=groups
        )

    line = gather(bundle, NZ, z_groups)

    def whole(part):
        got = gather(part, NY, y_groups)
        got = got.reshape(32, *got.shape[2:])
        return unpack(jnp.swapaxes(got, 0, 1).reshape(got.shape[1], -1, LANES))

    piv = whole(line[:, :2])
    rows = whole(line[:, 2:]).reshape(2, 2, RAW, TILE)
    piv = swap_cores(piv, core)

    inv0 = inverse(build(piv[0][0], True))
    pivot_row1 = build(piv[1][0], False).astype(BF)
    mult_p1 = dot(build(piv[0][1], False).astype(BF), inv0).astype(BF)
    inv1 = inverse(build(piv[1][1], True) - dot(mult_p1, pivot_row1))

    mult = []
    for s in range(2):
        first = dot(build(cols[0][s], held[s] == 0).astype(BF), inv0).astype(BF)
        second = build(cols[1][s], held[s] == 1) - jnp.where(held[s] > 0, dot(first, pivot_row1), 0.0)
        mult.append((first, dot(second.astype(BF), inv1).astype(BF)))
    out = []
    for t in range(2):
        j = t * 8 + col
        row0 = build(rows[0, t], j == 0).astype(BF)
        row1 = build(rows[1, t], j == 1) - jnp.where(j > 0, dot(mult_p1, row0), 0.0)
        row1 = row1.astype(BF)
        for s in range(2):
            tile = build(raw[s, t], held[s] == j)
            tile = tile - jnp.where((held[s] > 0) & (j > 0), dot(mult[s][0], row0), 0.0)
            tile = tile - jnp.where((held[s] > 1) & (j > 1), dot(mult[s][1], row1), 0.0)
            out.append(tile.astype(BF))
    out = jnp.stack([out[0], out[2], out[1], out[3]])
    return out.reshape(2, 2, 1, TILE, TILE)


def solution(mesh):
    return jax.shard_map(
        body,
        mesh=mesh,
        in_specs=(
            P("row", None, "col", None, None),
            P("row", None, "col", None, None),
            P("row", None, "col", None, None),
            P("row", None, "col"),
            P("row", None, "col"),
            P(),
        ),
        out_specs=P("row", None, "col", None, None),
        check_vma=False,
    )
```

```python
import functools
import math

import jax
import jax.numpy as jnp
from jax import lax
from jax.experimental import pallas as pl
from jax.experimental.pallas import tpu as pltpu
from jax.sharding import PartitionSpec as P

TILE = 512
KMAX = 64
LANES = 128
WIDE = TILE + LANES
BLOCKS = TILE // LANES
CHUNK = 16
PARTS = TILE // CHUNK
SHIFT = 1.1 * math.sqrt(TILE)
NY, NZ, NX = 4, 8, 4
BF = jnp.bfloat16
F32 = jnp.float32

SMEM = pl.BlockSpec(memory_space=pltpu.SMEM)
VMEM = pl.BlockSpec(memory_space=pltpu.VMEM)
PARAMS = pltpu.CompilerParams(vmem_limit_bytes=40 << 20)


def dot(a, b):
    return jnp.dot(a, b, preferred_element_type=F32)


def split(a):
    high = a.astype(BF)
    return high, (a - high.astype(F32)).astype(BF)


def dot_hi(a, b):
    return dot(a[0], b[0]) + (dot(a[0], b[1]) + dot(a[1], b[0]))


def eye():
    rows = lax.broadcasted_iota(jnp.int32, (TILE, TILE), 0)
    cols = lax.broadcasted_iota(jnp.int32, (TILE, TILE), 1)
    return (rows == cols).astype(F32)


def low_rank(left, right):
    return lax.dot_general(left, right, (((0,), (0,)), ((), ())), preferred_element_type=F32)


def build(wide, diag):
    factors = wide[:, TILE:].reshape(BLOCKS, 2, KMAX, LANES)
    left = jnp.concatenate([factors[k, 0] for k in range(BLOCKS)], axis=1)
    right = jnp.concatenate([factors[k, 1] for k in range(BLOCKS)], axis=1)
    tile = wide[:, :TILE].astype(F32) + low_rank(left, right)
    return tile + jnp.where(diag, SHIFT, 0.0) * eye()


def inverse(pivot):
    ident = eye()
    e = ident - pivot * (1.0 / SHIFT)
    es = split(e)
    e2 = dot_hi(es, es)
    e2s = split(e2)
    total = split(ident + e + e2 + dot_hi(es, e2s))
    e4 = dot_hi(e2s, e2s)
    whole = total[0].astype(F32) + total[1].astype(F32) + dot_hi(total, split(e4))
    return (whole * (1.0 / SHIFT)).astype(BF)


def kept_left(u, rank):
    rows = lax.broadcasted_iota(jnp.int32, (KMAX, TILE), 0)
    return jnp.where(rows < rank, u.astype(F32), 0.0).astype(BF)


def wide_tile(near, u, v, mask, rank):
    near = near * mask.astype(F32).astype(BF)
    left = kept_left(u, rank)
    factors = []
    for k in range(BLOCKS):
        cut = slice(k * LANES, (k + 1) * LANES)
        factors += [left[:, cut], v[:, cut]]
    return near, jnp.concatenate(factors, axis=0)


def head_kernel(slot, mask, ranks, near, u, v, cols, send):
    for s in range(2):
        near_part, factors = wide_tile(near[s, 0], u[s, 0], v[s, 0], mask[s, 0], ranks[s, 0])
        cols[s, :, :TILE] = near_part
        cols[s, :, TILE:] = factors
    s = slot[0]
    for t in range(2):
        near_part, factors = wide_tile(near[s, t], u[s, t], v[s, t], mask[s, t], ranks[s, t])
        send[:, t, :, :TILE] = near_part.reshape(PARTS, CHUNK, TILE)
        send[:, t, :, TILE:] = factors.reshape(PARTS, CHUNK, LANES)


def head(slot, mask, ranks, near, u, v):
    return pl.pallas_call(
        head_kernel,
        out_shape=(
            jax.ShapeDtypeStruct((2, TILE, WIDE), BF),
            jax.ShapeDtypeStruct((PARTS, 2, CHUNK, WIDE), BF),
        ),
        in_specs=[SMEM] * 3 + [VMEM] * 3,
        out_specs=(VMEM, VMEM),
        compiler_params=PARAMS,
        name="head",
    )(slot.reshape(1), mask, ranks, near, u, v)


def chain_kernel(place, held, own, other, cols_own, cols_other, out, piv, cols):
    core = place[0]
    piv[core] = own[...]
    piv[1 - core] = other[...]
    cols[core] = cols_own[...]
    cols[1 - core] = cols_other[...]

    def pivot(j, k):
        return build(piv[j, :, :, k].reshape(TILE, WIDE), j == k)

    inv0 = inverse(pivot(0, 0))
    row1 = pivot(1, 0).astype(BF)
    mult_p1 = dot(pivot(0, 1).astype(BF), inv0).astype(BF)
    inv1 = inverse(pivot(1, 1) - dot(mult_p1, row1))
    out[0] = mult_p1
    for s in range(2):
        first = dot(build(cols[0, s], held[s] == 0).astype(BF), inv0).astype(BF)
        second = build(cols[1, s], held[s] == 1)
        second = second - jnp.where(held[s] > 0, 1.0, 0.0) * dot(first, row1)
        out[1 + 2 * s] = first
        out[2 + 2 * s] = dot(second.astype(BF), inv1).astype(BF)


def chain(place, held, own, other, cols_own, cols_other):
    return pl.pallas_call(
        chain_kernel,
        out_shape=jax.ShapeDtypeStruct((5, TILE, TILE), BF),
        in_specs=[SMEM] * 2 + [VMEM] * 4,
        out_specs=VMEM,
        scratch_shapes=[
            pltpu.VMEM((2, NY, NZ, 2, CHUNK, WIDE), BF),
            pltpu.VMEM((2, 2, TILE, WIDE), BF),
        ],
        compiler_params=PARAMS,
        cost_estimate=pl.CostEstimate(
            flops=38 * 2 * TILE**3, bytes_accessed=8 << 20, transcendentals=0
        ),
        name="chain",
    )(place, held, own, other, cols_own, cols_other)


def last_kernel(place, held, mask, ranks, near, u, v, rows, mult, out):
    col = place[1]
    for t in range(2):
        j = t * 2 * NX + col
        row0 = build(rows[:, :, t].reshape(TILE, WIDE), j == 0).astype(BF)
        row1 = build(rows[:, :, 2 + t].reshape(TILE, WIDE), j == 1)
        row1 = (row1 - jnp.where(j > 0, 1.0, 0.0) * dot(mult[0], row0)).astype(BF)
        for s in range(2):
            tile = near[s, t].astype(F32) * mask[s, t].astype(F32)
            tile = tile + low_rank(kept_left(u[s, t], ranks[s, t]), v[s, t])
            tile = tile + jnp.where(held[s] == j, SHIFT, 0.0) * eye()
            for k, row in enumerate((row0, row1)):
                live = jnp.where((held[s] > k) & (j > k), 1.0, 0.0)
                tile = tile - live * dot(mult[1 + 2 * s + k], row)
            out[s, t] = tile.astype(BF)


def last(place, held, mask, ranks, near, u, v, rows, mult):
    return pl.pallas_call(
        last_kernel,
        out_shape=jax.ShapeDtypeStruct((2, 2, TILE, TILE), BF),
        in_specs=[SMEM] * 4 + [VMEM] * 5,
        out_specs=VMEM,
        compiler_params=PARAMS,
        cost_estimate=pl.CostEstimate(
            flops=16 * 2 * TILE**3, bytes_accessed=10 << 20, transcendentals=0
        ),
        name="last",
    )(place, held, mask, ranks, near, u, v, rows, mult)


def pairs(source, target):
    return [(source * 2 + core, target * 2 + core) for core in range(2)]


def body(near_tiles, basis_u, basis_v, near_mask, ranks, row_map):
    row = lax.axis_index("row")
    col = lax.axis_index("col")
    x, core = col // 2, col % 2
    place = jnp.stack([core, col])
    near = near_tiles.reshape(2, 2, TILE, TILE)
    u = basis_u.reshape(2, 2, KMAX, TILE)
    v = basis_v.reshape(2, 2, KMAX, TILE)
    mask = near_mask.reshape(2, 2)
    ranks = ranks.reshape(2, 2)
    slots = jnp.arange(64, dtype=jnp.int32)
    owner = [jnp.sum(jnp.where(row_map == k, slots, 0)) for k in range(2)]
    owner_row = [o // 2 for o in owner]
    held = lax.dynamic_slice_in_dim(row_map, row * 2, 2)

    slot = jnp.where(row == owner_row[0], owner[0], owner[1]) % 2
    cols, send = head(slot, mask, ranks, near, u, v)

    def first_hop(cols):
        return [lax.ppermute(cols, "col", pairs(0, to)) for to in (1, 3)]

    def take(got, k):
        return lax.dynamic_index_in_dim(got, owner_row[k], 0, keepdims=False)

    def apart():
        hop = first_hop(cols)
        again = head(owner[1] % 2, mask, ranks, near, u, v)[1]
        got = [lax.all_to_all(part, "row", 0, 0) for part in (send, again)]
        return jnp.stack([take(got[k], k) for k in range(2)]), hop

    def merged():
        hop = first_hop(cols)
        got = lax.all_to_all(send, "row", 0, 0)
        return jnp.stack([take(got, k) for k in range(2)]), hop

    chunk, hop = lax.cond(owner_row[0] == owner_row[1], apart, merged)

    pivots = chunk[:, 0]
    parts = [lax.ppermute(pivots, "col", pairs(0, to)) for to in (1, 3, 2)]
    pivots = jnp.where(x == 0, pivots, parts[0] + parts[1] + parts[2])

    cols = jnp.where(x == 0, cols, hop[0] + hop[1])
    hop = [lax.ppermute(cols[s], "col", pairs(source, 2)) for s, source in enumerate((1, 3))]
    cols = jnp.where(x == 2, jnp.stack(hop), cols)
    swap = [(c, c ^ 1) for c in range(2 * NX)]
    cols_other = lax.ppermute(cols, "col", swap)

    z_groups = [[y * NZ + z for z in range(NZ)] for y in range(NY)]
    y_groups = [[y * NZ + z for y in range(NY)] for z in range(NZ)]

    def gather(value, count, groups):
        return lax.all_to_all(
            jnp.broadcast_to(value[None], (count, *value.shape)), "row", 0, 0, axis_index_groups=groups
        )

    bundle = jnp.concatenate([pivots, chunk.reshape(4, CHUNK, WIDE)])
    line = gather(bundle, NZ, z_groups)
    piv = gather(line[:, :2], NY, y_groups)
    rows = gather(line[:, 2:], NY, y_groups)
    piv_other = lax.ppermute(piv, "col", swap)
    mult = chain(place, held, piv, piv_other, cols, cols_other)
    out = last(place, held, mask, ranks, near, u, v, rows, mult)
    return out.reshape(2, 2, 1, TILE, TILE)


def solution(mesh):
    return jax.shard_map(
        body,
        mesh=mesh,
        in_specs=(
            P("row", None, "col", None, None),
            P("row", None, "col", None, None),
            P("row", None, "col", None, None),
            P("row", None, "col"),
            P("row", None, "col"),
            P(),
        ),
        out_specs=P("row", None, "col", None, None),
        check_vma=False,
    )
```

```python
import math

import jax
import jax.numpy as jnp
from jax import lax
from jax.experimental import pallas as pl
from jax.experimental.pallas import tpu as pltpu
from jax.sharding import PartitionSpec as P

TILE = 512
KMAX = 64
LANES = 128
WIDE = TILE + LANES
PAIR = TILE + WIDE
BLOCKS = TILE // LANES
CHUNK = 16
PARTS = TILE // CHUNK
NROWS = 64
SHIFT = 1.1 * math.sqrt(TILE)
NY, NZ, NX = 4, 8, 4
BF = jnp.bfloat16
F32 = jnp.float32

SMEM = pl.BlockSpec(memory_space=pltpu.SMEM)
VMEM = pl.BlockSpec(memory_space=pltpu.VMEM)
ANY = pl.BlockSpec(memory_space=pl.ANY)
PARAMS = pltpu.CompilerParams(vmem_limit_bytes=40 << 20)


def dot(a, b):
    return jnp.dot(a, b, preferred_element_type=F32)


def split(a):
    high = a.astype(BF)
    return high, (a - high.astype(F32)).astype(BF)


def dot_hi(a, b):
    return dot(a[0], b[0]) + (dot(a[0], b[1]) + dot(a[1], b[0]))


def eye():
    rows = lax.broadcasted_iota(jnp.int32, (TILE, TILE), 0)
    cols = lax.broadcasted_iota(jnp.int32, (TILE, TILE), 1)
    return (rows == cols).astype(F32)


def low_rank(left, right):
    return lax.dot_general(left, right, (((0,), (0,)), ((), ())), preferred_element_type=F32)


def build(wide, diag):
    factors = wide[:, TILE:].reshape(BLOCKS, 2, KMAX, LANES)
    left = jnp.concatenate([factors[k, 0] for k in range(BLOCKS)], axis=1)
    right = jnp.concatenate([factors[k, 1] for k in range(BLOCKS)], axis=1)
    tile = wide[:, :TILE].astype(F32) + low_rank(left, right)
    return tile + jnp.where(diag, SHIFT, 0.0) * eye()


def inverse(pivot):
    ident = eye()
    e = ident - pivot * (1.0 / SHIFT)
    es = split(e)
    e2 = dot_hi(es, es)
    e2s = split(e2)
    total = split(ident + e + e2 + dot_hi(es, e2s))
    e4 = dot_hi(e2s, e2s)
    whole = total[0].astype(F32) + total[1].astype(F32) + dot_hi(total, split(e4))
    return (whole * (1.0 / SHIFT)).astype(BF)


def kept_left(u, rank):
    rows = lax.broadcasted_iota(jnp.int32, (KMAX, TILE), 0)
    return jnp.where(rows < rank, u.astype(F32), 0.0).astype(BF)


def lane_blocks(left, right):
    parts = []
    for k in range(BLOCKS):
        cut = slice(k * LANES, (k + 1) * LANES)
        parts += [left[:, cut], right[:, cut]]
    return jnp.concatenate(parts, axis=0)


def find_owners(row_map):
    def step(slot, found):
        held = row_map[slot]
        return jnp.where(held == 0, slot, found[0]), jnp.where(held == 1, slot, found[1])

    return lax.fori_loop(0, NROWS, step, (0, 0), unroll=8)


def head_kernel(second, row_map, mask, ranks, near, u, v, cols, send):
    row = lax.axis_index("row")
    col = lax.axis_index("col")
    for s in range(2):
        cols[s, :, :TILE] = near[s, 0] * mask[s, 0].astype(F32).astype(BF)
        cols[s, :, TILE:] = lane_blocks(kept_left(u[s, 0], ranks[s, 0]), v[s, 0])
    owners = find_owners(row_map)
    panel = 1 if second else jnp.where(row == owners[0] >> 1, 0, 1)
    s = jnp.where(panel == 0, owners[0], owners[1]) & 1
    for t in range(2):
        low = low_rank(kept_left(u[s, t], ranks[s, t]), v[s, t])
        tile = (near[s, t].astype(F32) * mask[s, t].astype(F32) + low).astype(BF)
        start = t * WIDE
        send[:, :, start : start + TILE] = tile.reshape(PARTS, CHUNK, TILE)

    @pl.when(col == panel)
    def _():
        send[:, :, :WIDE] = cols[s].reshape(PARTS, CHUNK, WIDE)


def head(second, row_map, mask, ranks, near, u, v):
    def kernel(*refs):
        head_kernel(second, *refs)

    return pl.pallas_call(
        kernel,
        out_shape=(
            jax.ShapeDtypeStruct((2, TILE, WIDE), BF),
            jax.ShapeDtypeStruct((PARTS, CHUNK, WIDE + TILE), BF),
        ),
        in_specs=[SMEM] * 3 + [VMEM] * 3,
        out_specs=(VMEM, VMEM),
        compiler_params=PARAMS,
        name="head_again" if second else "head",
    )(row_map, mask, ranks, near, u, v)


def take_kernel(row_map, got0, got1, pivots, rows, chunk, sems):
    copies = []
    for k, (got, owner) in enumerate(zip((got0, got1), find_owners(row_map))):
        copies.append(pltpu.make_async_copy(got.at[owner >> 1], chunk.at[k], sems.at[k]))
        copies[-1].start()
    for copy in copies:
        copy.wait()
    core = lax.axis_index("col") & 1
    pivots[:, :TILE] = chunk[1 - core, :, :TILE]
    pivots[:, TILE:] = chunk[core, :, :WIDE]
    for t in range(2):
        for k in range(2):
            rows[:, (2 * t + k) * TILE : (2 * t + k + 1) * TILE] = chunk[k, :, t * WIDE : t * WIDE + TILE]


def take(row_map, got0, got1):
    return pl.pallas_call(
        take_kernel,
        out_shape=(
            jax.ShapeDtypeStruct((CHUNK, PAIR), BF),
            jax.ShapeDtypeStruct((CHUNK, 4 * TILE), BF),
        ),
        in_specs=[SMEM, ANY, ANY],
        out_specs=(VMEM, VMEM),
        scratch_shapes=[pltpu.VMEM((2, CHUNK, WIDE + TILE), BF), pltpu.SemaphoreType.DMA((2,))],
        compiler_params=PARAMS,
        name="take",
    )(row_map, got0, got1)


def bundle_kernel(own, hop1, hop3, hop2, rows, out):
    x = lax.axis_index("col") >> 1

    @pl.when(x == 0)
    def _():
        for z in range(NZ):
            out[z, :, :PAIR] = own[...]

    @pl.when(x != 0)
    def _():
        pivots = hop1[...] + hop3[...] + hop2[...]
        for z in range(NZ):
            out[z, :, :PAIR] = pivots

    for z in range(NZ):
        out[z, :, PAIR:] = rows[...]


def bundle(own, hops, rows):
    return pl.pallas_call(
        bundle_kernel,
        out_shape=jax.ShapeDtypeStruct((NZ, CHUNK, PAIR + 4 * TILE), BF),
        in_specs=[VMEM] * 5,
        out_specs=VMEM,
        compiler_params=PARAMS,
        name="bundle",
    )(own, *hops, rows)


def chain_kernel(own, other, out, piv):
    core = lax.axis_index("col") & 1
    piv[core] = own[...].reshape(TILE, PAIR)
    piv[1 - core] = other[...].reshape(TILE, PAIR)
    inv0 = inverse(build(piv[0, :, TILE:], True))
    row1 = piv[1, :, :TILE]
    mult_p1 = dot(piv[0, :, :TILE], inv0).astype(BF)
    out[0] = inv0
    out[1] = row1
    out[2] = mult_p1
    out[3] = inverse(build(piv[1, :, TILE:], True) - dot(mult_p1, row1))


def chain(own, other):
    return pl.pallas_call(
        chain_kernel,
        out_shape=jax.ShapeDtypeStruct((4, TILE, TILE), BF),
        in_specs=[VMEM] * 2,
        out_specs=VMEM,
        scratch_shapes=[pltpu.VMEM((2, TILE, PAIR), BF)],
        compiler_params=PARAMS,
        cost_estimate=pl.CostEstimate(flops=28 * 2 * TILE**3, bytes_accessed=5 << 20, transcendentals=0),
        name="chain",
    )(own, other)


def mults_kernel(row_map, own, other, lead, out, cols):
    core = lax.axis_index("col") & 1
    row = lax.axis_index("row")
    cols[core] = own[...]
    cols[1 - core] = other[...]
    for s in range(2):
        held = row_map[2 * row + s]
        first = dot(build(cols[0, s], held == 0).astype(BF), lead[0]).astype(BF)
        second = build(cols[1, s], held == 1)
        second = jnp.where(held > 0, second - dot(first, lead[1]), second)
        out[s, 0] = first
        out[s, 1] = dot(second.astype(BF), lead[3]).astype(BF)


def mults(row_map, own, other, lead):
    return pl.pallas_call(
        mults_kernel,
        out_shape=jax.ShapeDtypeStruct((2, 2, TILE, TILE), BF),
        in_specs=[SMEM] + [VMEM] * 3,
        out_specs=VMEM,
        scratch_shapes=[pltpu.VMEM((2, 2, TILE, WIDE), BF)],
        compiler_params=PARAMS,
        cost_estimate=pl.CostEstimate(flops=7 * 2 * TILE**3, bytes_accessed=7 << 20, transcendentals=0),
        name="mults",
    )(row_map, own, other, lead)


def last_kernel(row_map, mask, ranks, near, u, v, rows, lead, mult, out):
    row = lax.axis_index("row")
    col = lax.axis_index("col")
    t = pl.program_id(0)
    j = t * 2 * NX + col
    row0 = rows[:, :, :, :TILE].reshape(TILE, TILE).astype(F32)
    row0 = jnp.where(j == 1, lead[1].astype(F32), row0).astype(BF)
    row1 = rows[:, :, :, TILE:].reshape(TILE, TILE).astype(F32)
    row1 = (row1 - dot(lead[2], row0)).astype(BF)
    for s in range(2):
        held = row_map[2 * row + s]
        tile = near[s, 0].astype(F32) * mask[s, t].astype(F32)
        tile = tile + low_rank(kept_left(u[s, 0], ranks[s, t]), v[s, 0])
        tile = tile + jnp.where(held == j, SHIFT, 0.0) * eye()
        for k, pivot_row in enumerate((row0, row1)):
            live = (held > k) & (j > k)
            tile = jnp.where(live, tile - dot(mult[s, k], pivot_row), tile)
        out[s, 0] = tile.astype(BF)


def last(row_map, mask, ranks, near, u, v, rows, lead, mult):
    def tiles(height):
        return pl.BlockSpec((2, 1, height, TILE), lambda t: (0, t, 0, 0))

    return pl.pallas_call(
        last_kernel,
        grid=(2,),
        out_shape=jax.ShapeDtypeStruct((2, 2, TILE, TILE), BF),
        in_specs=[SMEM] * 3
        + [tiles(TILE), tiles(KMAX), tiles(KMAX)]
        + [pl.BlockSpec((NY, NZ, CHUNK, 2 * TILE), lambda t: (0, 0, 0, t)), VMEM, VMEM],
        out_specs=tiles(TILE),
        compiler_params=PARAMS,
        cost_estimate=pl.CostEstimate(flops=12 * 2 * TILE**3, bytes_accessed=10 << 20, transcendentals=0),
        name="last",
    )(row_map, mask, ranks, near, u, v, rows, lead, mult)


def pairs(source, target):
    return [(source * 2 + core, target * 2 + core) for core in range(2)]


def body(near_tiles, basis_u, basis_v, near_mask, ranks, row_map):
    near = near_tiles.reshape(2, 2, TILE, TILE)
    u = basis_u.reshape(2, 2, KMAX, TILE)
    v = basis_v.reshape(2, 2, KMAX, TILE)
    mask = near_mask.reshape(2, 2)
    ranks = ranks.reshape(2, 2)
    x = lax.axis_index("col") >> 1

    cols, send = head(False, row_map, mask, ranks, near, u, v)

    def scatter(part):
        return lax.all_to_all(part, "row", 0, 0)

    def first_hop(cols):
        return [lax.ppermute(cols, "col", pairs(0, to)) for to in (1, 3)]

    def apart():
        again = head(True, row_map, mask, ranks, near, u, v)[1]
        hop = first_hop(cols)
        return take(row_map, scatter(send), scatter(again)), hop

    def merged():
        hop = first_hop(cols)
        got = scatter(send)
        return take(row_map, got, got), hop

    one_device = jnp.any(row_map.reshape(-1, 2).sum(axis=1) == 1)
    (own, rows), hop = lax.cond(one_device, apart, merged)

    hops = [lax.ppermute(own, "col", pairs(0, to)) for to in (1, 3, 2)]
    line = bundle(own, hops, rows)

    cols = jnp.where(x == 0, cols, hop[0] + hop[1])
    hop = [lax.ppermute(cols[s], "col", pairs(source, 2)) for s, source in enumerate((1, 3))]
    cols = jnp.where(x == 2, jnp.stack(hop), cols)
    swap = [(c, c ^ 1) for c in range(2 * NX)]

    z_groups = [[y * NZ + z for z in range(NZ)] for y in range(NY)]
    y_groups = [[y * NZ + z for y in range(NY)] for z in range(NZ)]
    line = lax.all_to_all(line, "row", 0, 0, axis_index_groups=z_groups)

    def gather(part):
        part = jnp.broadcast_to(part[None], (NY, *part.shape))
        return lax.all_to_all(part, "row", 0, 0, axis_index_groups=y_groups)

    piv = gather(line[:, :, :PAIR])
    rows = gather(line[:, :, PAIR:])
    lead = chain(piv, lax.ppermute(piv, "col", swap))
    mult = mults(row_map, cols, lax.ppermute(cols, "col", swap), lead)
    out = last(row_map, mask, ranks, near, u, v, rows, lead, mult)
    return out.reshape(2, 2, 1, TILE, TILE)


def solution(mesh):
    return jax.shard_map(
        body,
        mesh=mesh,
        in_specs=(
            P("row", None, "col", None, None),
            P("row", None, "col", None, None),
            P("row", None, "col", None, None),
            P("row", None, "col"),
            P("row", None, "col"),
            P(),
        ),
        out_specs=P("row", None, "col", None, None),
        check_vma=False,
    )
```

```python
import math

import jax
import jax.numpy as jnp
from jax import lax
from jax.experimental import pallas as pl
from jax.experimental.pallas import tpu as pltpu
from jax.sharding import PartitionSpec as P

TILE = 512
KMAX = 64
LANES = 128
WIDE = TILE + LANES
FIRST = TILE + WIDE
BLOCKS = TILE // LANES
CHUNK = 16
PARTS = TILE // CHUNK
NROWS = 64
SHIFT = 1.1 * math.sqrt(TILE)
NY, NZ, NX = 4, 8, 4
BF = jnp.bfloat16
F32 = jnp.float32

SMEM = pl.BlockSpec(memory_space=pltpu.SMEM)
VMEM = pl.BlockSpec(memory_space=pltpu.VMEM)
ANY = pl.BlockSpec(memory_space=pl.ANY)
PARAMS = pltpu.CompilerParams(vmem_limit_bytes=40 << 20)


def dot(a, b):
    return jnp.dot(a, b, preferred_element_type=F32)


def split(a):
    high = a.astype(BF)
    return high, (a - high.astype(F32)).astype(BF)


def dot_hi(a, b):
    return dot(a[0], b[0]) + (dot(a[0], b[1]) + dot(a[1], b[0]))


def eye():
    rows = lax.broadcasted_iota(jnp.int32, (TILE, TILE), 0)
    cols = lax.broadcasted_iota(jnp.int32, (TILE, TILE), 1)
    return (rows == cols).astype(F32)


def low_rank(left, right):
    return lax.dot_general(left, right, (((0,), (0,)), ((), ())), preferred_element_type=F32)


def build(near, factors, diag):
    factors = factors.reshape(BLOCKS, 2, KMAX, LANES)
    left = jnp.concatenate([factors[k, 0] for k in range(BLOCKS)], axis=1)
    right = jnp.concatenate([factors[k, 1] for k in range(BLOCKS)], axis=1)
    tile = near.astype(F32) + low_rank(left, right)
    return tile + jnp.where(diag, SHIFT, 0.0) * eye()


def inverse(pivot):
    ident = eye()
    e = ident - pivot * (1.0 / SHIFT)
    es = split(e)
    e2 = dot_hi(es, es)
    e2s = split(e2)
    total = split(ident + e + e2 + dot_hi(es, e2s))
    e4 = dot_hi(e2s, e2s)
    whole = total[0].astype(F32) + total[1].astype(F32) + dot_hi(total, split(e4))
    return (whole * (1.0 / SHIFT)).astype(BF)


def kept_left(u, rank):
    rows = lax.broadcasted_iota(jnp.int32, (KMAX, TILE), 0)
    return jnp.where(rows < rank, u.astype(F32), 0.0).astype(BF)


def lane_blocks(left, right):
    parts = []
    for k in range(BLOCKS):
        cut = slice(k * LANES, (k + 1) * LANES)
        parts += [left[:, cut], right[:, cut]]
    return jnp.concatenate(parts, axis=0)


def find_owners(row_map):
    def step(slot, found):
        held = row_map[slot]
        return jnp.where(held == 0, slot, found[0]), jnp.where(held == 1, slot, found[1])

    return lax.fori_loop(0, NROWS, step, (0, 0), unroll=8)


def head_kernel(second, row_map, mask, ranks, near, u, v, send, near_buf, u_buf, v_buf, sems):
    row = lax.axis_index("row")
    col = lax.axis_index("col")
    owners = find_owners(row_map)
    panel = 1 if second else jnp.where(row == owners[0] >> 1, 0, 1)
    s = jnp.where(panel == 0, owners[0], owners[1]) & 1
    copies = [
        pltpu.make_async_copy(source.at[s], target, sems.at[i])
        for i, (source, target) in enumerate(((u, u_buf), (v, v_buf), (near, near_buf)))
    ]
    for copy in copies:
        copy.start()
    for copy in copies:
        copy.wait()
    for t in range(2):
        low = low_rank(kept_left(u_buf[t], ranks[s, t]), v_buf[t])
        tile = (near_buf[t].astype(F32) * mask[s, t].astype(F32) + low).astype(BF)
        start = t * WIDE
        send[:, :, start : start + TILE] = tile.reshape(PARTS, CHUNK, TILE)

    @pl.when(col == panel)
    def _():
        tile = near_buf[0] * mask[s, 0].astype(F32).astype(BF)
        factors = lane_blocks(kept_left(u_buf[0], ranks[s, 0]), v_buf[0])
        send[:, :, :TILE] = tile.reshape(PARTS, CHUNK, TILE)
        send[:, :, TILE:WIDE] = factors.reshape(PARTS, CHUNK, LANES)


def head(second, row_map, mask, ranks, near, u, v):
    def kernel(*refs):
        head_kernel(second, *refs)

    return pl.pallas_call(
        kernel,
        out_shape=jax.ShapeDtypeStruct((PARTS, CHUNK, WIDE + TILE), BF),
        in_specs=[SMEM] * 3 + [ANY] * 3,
        out_specs=VMEM,
        scratch_shapes=[
            pltpu.VMEM((2, TILE, TILE), BF),
            pltpu.VMEM((2, KMAX, TILE), BF),
            pltpu.VMEM((2, KMAX, TILE), BF),
            pltpu.SemaphoreType.DMA((3,)),
        ],
        compiler_params=PARAMS,
        name="head_again" if second else "head",
    )(row_map, mask, ranks, near, u, v)


def columns_kernel(mask, ranks, near, u, v, cols):
    for s in range(2):
        cols[s, :, :TILE] = near[s, 0] * mask[s, 0].astype(F32).astype(BF)
        cols[s, :, TILE:] = lane_blocks(kept_left(u[s, 0], ranks[s, 0]), v[s, 0])


def columns(mask, ranks, near, u, v):
    def tiles(height):
        return pl.BlockSpec((2, 1, height, TILE), lambda i: (0, 0, 0, 0))

    return pl.pallas_call(
        columns_kernel,
        grid=(1,),
        out_shape=jax.ShapeDtypeStruct((2, TILE, WIDE), BF),
        in_specs=[SMEM] * 2 + [tiles(TILE), tiles(KMAX), tiles(KMAX)],
        out_specs=pl.BlockSpec((2, TILE, WIDE), lambda i: (0, 0, 0)),
        compiler_params=PARAMS,
        name="columns",
    )(mask, ranks, near, u, v)


def take_kernel(row_map, got0, got1, out, chunk, sems):
    copies = []
    for k, (got, owner) in enumerate(zip((got0, got1), find_owners(row_map))):
        copies.append(pltpu.make_async_copy(got.at[owner >> 1], chunk.at[k], sems.at[k]))
        copies[-1].start()
    for copy in copies:
        copy.wait()
    core = lax.axis_index("col") & 1
    parts = [chunk[0, :, :TILE], chunk[1, :, :TILE], chunk[core, :, TILE:WIDE]]
    parts += [chunk[0, :, WIDE:], chunk[1, :, WIDE:]]
    whole = jnp.concatenate(parts, axis=1)
    for z in range(NZ):
        out[z] = whole


def take(row_map, got0, got1):
    return pl.pallas_call(
        take_kernel,
        out_shape=jax.ShapeDtypeStruct((NZ, CHUNK, FIRST + 2 * TILE), BF),
        in_specs=[SMEM, ANY, ANY],
        out_specs=VMEM,
        scratch_shapes=[pltpu.VMEM((2, CHUNK, WIDE + TILE), BF), pltpu.SemaphoreType.DMA((2,))],
        compiler_params=PARAMS,
        name="take",
    )(row_map, got0, got1)


def fan_kernel(line, pivots, rows0, rows1):
    pivots[...] = line[:, :, :FIRST]
    for y in range(NY):
        rows0[y] = line[:, :, : 2 * TILE]
        rows1[y] = line[:, :, FIRST:]


def fan(line):
    rows = jax.ShapeDtypeStruct((NY, NZ, CHUNK, 2 * TILE), BF)
    return pl.pallas_call(
        fan_kernel,
        out_shape=(jax.ShapeDtypeStruct((NZ, CHUNK, FIRST), BF), rows, rows),
        in_specs=[VMEM],
        out_specs=(VMEM,) * 3,
        compiler_params=PARAMS,
        name="fan",
    )(line)


def fan_pivots_kernel(own, hop1, hop3, hop2, out):
    x = lax.axis_index("col") >> 1

    @pl.when(x == 0)
    def _():
        for y in range(NY):
            out[y] = own[...]

    @pl.when(x != 0)
    def _():
        pivots = hop1[...] + hop3[...] + hop2[...]
        for y in range(NY):
            out[y] = pivots


def fan_pivots(own, hops):
    return pl.pallas_call(
        fan_pivots_kernel,
        out_shape=jax.ShapeDtypeStruct((NY, NZ, CHUNK, FIRST), BF),
        in_specs=[VMEM] * 4,
        out_specs=VMEM,
        compiler_params=PARAMS,
        name="fan_pivots",
    )(own, *hops)


def chain_kernel(own, other, out, piv):
    core = lax.axis_index("col") & 1
    piv[core] = own[...].reshape(TILE, FIRST)
    piv[1 - core] = other[...].reshape(TILE, FIRST)
    inv0 = inverse(build(piv[0, :, :TILE], piv[0, :, 2 * TILE :], True))
    row1 = piv[1, :, :TILE]
    mult_p1 = dot(piv[0, :, TILE : 2 * TILE], inv0).astype(BF)
    out[0] = inv0
    out[1] = row1
    out[2] = mult_p1
    pivot = build(piv[1, :, TILE : 2 * TILE], piv[1, :, 2 * TILE :], True)
    out[3] = inverse(pivot - dot(mult_p1, row1))


def chain(own, other):
    return pl.pallas_call(
        chain_kernel,
        out_shape=jax.ShapeDtypeStruct((4, TILE, TILE), BF),
        in_specs=[VMEM] * 2,
        out_specs=VMEM,
        scratch_shapes=[pltpu.VMEM((2, TILE, FIRST), BF)],
        compiler_params=PARAMS,
        cost_estimate=pl.CostEstimate(flops=28 * 2 * TILE**3, bytes_accessed=5 << 20, transcendentals=0),
        name="chain",
    )(own, other)


def mults_kernel(row_map, own, other, lead, out, cols):
    core = lax.axis_index("col") & 1
    row = lax.axis_index("row")
    cols[core] = own[...]
    cols[1 - core] = other[...]
    for s in range(2):
        held = row_map[2 * row + s]
        first = build(cols[0, s, :, :TILE], cols[0, s, :, TILE:], held == 0).astype(BF)
        first = dot(first, lead[0]).astype(BF)
        second = build(cols[1, s, :, :TILE], cols[1, s, :, TILE:], held == 1)
        second = jnp.where(held > 0, second - dot(first, lead[1]), second)
        out[s, 0] = first
        out[s, 1] = dot(second.astype(BF), lead[3]).astype(BF)


def mults(row_map, own, other, lead):
    return pl.pallas_call(
        mults_kernel,
        out_shape=jax.ShapeDtypeStruct((2, 2, TILE, TILE), BF),
        in_specs=[SMEM] + [VMEM] * 3,
        out_specs=VMEM,
        scratch_shapes=[pltpu.VMEM((2, 2, TILE, WIDE), BF)],
        compiler_params=PARAMS,
        cost_estimate=pl.CostEstimate(flops=7 * 2 * TILE**3, bytes_accessed=7 << 20, transcendentals=0),
        name="mults",
    )(row_map, own, other, lead)


def last_kernel(
    row_map, mask, ranks, near, u, v, rows0, rows1, lead, mult, out,
    near_buf, u_buf, v_buf, rows_buf, lead_buf, mult_buf, out_buf, sems, out_sems,
):
    row = lax.axis_index("row")
    col = lax.axis_index("col")
    moves = {
        "lead": (lead.at[pl.ds(1, 2)], lead_buf),
        "rows1": (rows1, rows_buf.at[1]),
        "u": (u, u_buf),
        "v": (v, v_buf),
        "near1": (near.at[:, 1], near_buf.at[1]),
        "mult": (mult, mult_buf),
        "rows0": (rows0, rows_buf.at[0]),
        "near0": (near.at[:, 0], near_buf.at[0]),
    }
    copies = {}
    for i, (name, (source, target)) in enumerate(moves.items()):
        copies[name] = pltpu.make_async_copy(source, target, sems.at[i])
        copies[name].start()
    stores = []
    for t in (1, 0):
        j = t * 2 * NX + col
        if t == 1:
            copies["lead"].wait()
        copies[f"rows{t}"].wait()
        row0 = rows_buf[t, :, :, :, :TILE].reshape(TILE, TILE)
        if t == 0:
            row0 = jnp.where(j == 1, lead_buf[0].astype(F32), row0.astype(F32)).astype(BF)
        row1 = rows_buf[t, :, :, :, TILE:].reshape(TILE, TILE).astype(F32)
        row1 = (row1 - dot(lead_buf[1], row0)).astype(BF)
        for name in ("u", "v", "near1", "mult") if t == 1 else ("near0",):
            copies[name].wait()
        for s in range(2):
            held = row_map[2 * row + s]
            tile = near_buf[t, s].astype(F32) * mask[s, t].astype(F32)
            tile = tile + low_rank(kept_left(u_buf[s, t], ranks[s, t]), v_buf[s, t])
            tile = tile + jnp.where(held == j, SHIFT, 0.0) * eye()
            for k, pivot_row in enumerate((row0, row1)):
                live = (held > k) & (j > k)
                tile = jnp.where(live, tile - dot(mult_buf[s, k], pivot_row), tile)
            out_buf[s, t] = tile.astype(BF)
            store = pltpu.make_async_copy(out_buf.at[s, t], out.at[s, t], out_sems.at[s, t])
            store.start()
            stores.append(store)
    for store in stores:
        store.wait()


def last(row_map, mask, ranks, near, u, v, rows0, rows1, lead, mult):
    return pl.pallas_call(
        last_kernel,
        out_shape=jax.ShapeDtypeStruct((2, 2, TILE, TILE), BF),
        in_specs=[SMEM] * 3 + [ANY] * 7,
        out_specs=ANY,
        scratch_shapes=[
            pltpu.VMEM((2, 2, TILE, TILE), BF),
            pltpu.VMEM((2, 2, KMAX, TILE), BF),
            pltpu.VMEM((2, 2, KMAX, TILE), BF),
            pltpu.VMEM((2, NY, NZ, CHUNK, 2 * TILE), BF),
            pltpu.VMEM((2, TILE, TILE), BF),
            pltpu.VMEM((2, 2, TILE, TILE), BF),
            pltpu.VMEM((2, 2, TILE, TILE), BF),
            pltpu.SemaphoreType.DMA((8,)),
            pltpu.SemaphoreType.DMA((2, 2)),
        ],
        compiler_params=pltpu.CompilerParams(vmem_limit_bytes=56 << 20),
        cost_estimate=pl.CostEstimate(flops=12 * 2 * TILE**3, bytes_accessed=10 << 20, transcendentals=0),
        name="last",
    )(row_map, mask, ranks, near, u, v, rows0, rows1, lead, mult)


def pairs(source, target):
    return [(source * 2 + core, target * 2 + core) for core in range(2)]


def body(near_tiles, basis_u, basis_v, near_mask, ranks, row_map):
    near = near_tiles.reshape(2, 2, TILE, TILE)
    u = basis_u.reshape(2, 2, KMAX, TILE)
    v = basis_v.reshape(2, 2, KMAX, TILE)
    mask = near_mask.reshape(2, 2)
    ranks = ranks.reshape(2, 2)
    x = lax.axis_index("col") >> 1

    send = head(False, row_map, mask, ranks, near, u, v)

    def scatter(part):
        return lax.all_to_all(part, "row", 0, 0)

    def first_hop():
        cols = columns(mask, ranks, near, u, v)
        return [cols] + [lax.ppermute(cols, "col", pairs(0, to)) for to in (1, 3)]

    def apart():
        again = head(True, row_map, mask, ranks, near, u, v)
        got = [scatter(send), scatter(again)]
        return take(row_map, *got), first_hop()

    def merged():
        got = scatter(send)
        return take(row_map, got, got), first_hop()

    one_device = jnp.any(row_map.reshape(-1, 2).sum(axis=1) == 1)
    line, hop = lax.cond(one_device, apart, merged)

    cols = jnp.where(x == 0, hop[0], hop[1] + hop[2])
    hop = [lax.ppermute(cols[s], "col", pairs(source, 2)) for s, source in enumerate((1, 3))]
    cols = jnp.where(x == 2, jnp.stack(hop), cols)
    swap = [(c, c ^ 1) for c in range(2 * NX)]

    z_groups = [[y * NZ + z for z in range(NZ)] for y in range(NY)]
    y_groups = [[y * NZ + z for y in range(NY)] for z in range(NZ)]
    line = lax.all_to_all(line, "row", 0, 0, axis_index_groups=z_groups)

    def gather(part):
        return lax.all_to_all(part, "row", 0, 0, axis_index_groups=y_groups)

    pivots, rows0, rows1 = fan(line)
    rows1 = gather(rows1)
    hops = [lax.ppermute(pivots, "col", pairs(0, to)) for to in (1, 3, 2)]
    piv = gather(fan_pivots(pivots, hops))
    rows0, piv = lax.optimization_barrier((rows0, piv))
    rows0 = gather(rows0)
    lead = chain(piv, lax.ppermute(piv, "col", swap))
    mult = mults(row_map, cols, lax.ppermute(cols, "col", swap), lead)
    out = last(row_map, mask, ranks, near, u, v, rows0, rows1, lead, mult)
    return out.reshape(2, 2, 1, TILE, TILE)


def solution(mesh):
    return jax.shard_map(
        body,
        mesh=mesh,
        in_specs=(
            P("row", None, "col", None, None),
            P("row", None, "col", None, None),
            P("row", None, "col", None, None),
            P("row", None, "col"),
            P("row", None, "col"),
            P(),
        ),
        out_specs=P("row", None, "col", None, None),
        check_vma=False,
    )
```

```python
import math

import jax
import jax.numpy as jnp
from jax import lax
from jax.experimental import pallas as pl
from jax.experimental.pallas import tpu as pltpu
from jax.sharding import PartitionSpec as P

TILE = 512
KMAX = 64
LANES = 128
WIDE = TILE + LANES
FIRST = TILE + WIDE
BLOCKS = TILE // LANES
CHUNK = 16
PARTS = TILE // CHUNK
NROWS = 64
SHIFT = 1.1 * math.sqrt(TILE)
NY, NZ, NX = 4, 8, 4
BF = jnp.bfloat16
F32 = jnp.float32

SMEM = pl.BlockSpec(memory_space=pltpu.SMEM)
VMEM = pl.BlockSpec(memory_space=pltpu.VMEM)
ANY = pl.BlockSpec(memory_space=pl.ANY)
PARAMS = pltpu.CompilerParams(vmem_limit_bytes=32 << 20)
SMALL = pltpu.CompilerParams(vmem_limit_bytes=28 << 20)


def dot(a, b):
    return jnp.dot(a, b, preferred_element_type=F32)


def split(a):
    high = a.astype(BF)
    return high, (a - high.astype(F32)).astype(BF)


def dot_hi(a, b):
    return dot(a[0], b[0]) + (dot(a[0], b[1]) + dot(a[1], b[0]))


def eye():
    rows = lax.broadcasted_iota(jnp.int32, (TILE, TILE), 0)
    cols = lax.broadcasted_iota(jnp.int32, (TILE, TILE), 1)
    return (rows == cols).astype(F32)


def low_rank(left, right):
    return lax.dot_general(left, right, (((0,), (0,)), ((), ())), preferred_element_type=F32)


def build(near, factors, diag):
    factors = factors.reshape(BLOCKS, 2, KMAX, LANES)
    left = jnp.concatenate([factors[k, 0] for k in range(BLOCKS)], axis=1)
    right = jnp.concatenate([factors[k, 1] for k in range(BLOCKS)], axis=1)
    tile = near.astype(F32) + low_rank(left, right)
    return tile + jnp.where(diag, SHIFT, 0.0) * eye()


def inverse(pivot):
    ident = eye()
    e = ident - pivot * (1.0 / SHIFT)
    es = split(e)
    e2 = dot_hi(es, es)
    e2s = split(e2)
    total = split(ident + e + e2 + dot_hi(es, e2s))
    e4 = dot_hi(e2s, e2s)
    whole = total[0].astype(F32) + total[1].astype(F32) + dot_hi(total, split(e4))
    return (whole * (1.0 / SHIFT)).astype(BF)


def kept_left(u, rank):
    rows = lax.broadcasted_iota(jnp.int32, (KMAX, TILE), 0)
    return jnp.where(rows < rank, u.astype(F32), 0.0).astype(BF)


def lane_blocks(left, right):
    parts = []
    for k in range(BLOCKS):
        cut = slice(k * LANES, (k + 1) * LANES)
        parts += [left[:, cut], right[:, cut]]
    return jnp.concatenate(parts, axis=0)


def find_owners(row_map):
    def step(slot, found):
        held = row_map[slot]
        return jnp.where(held == 0, slot, found[0]), jnp.where(held == 1, slot, found[1])

    return lax.fori_loop(0, NROWS, step, (0, 0), unroll=8)


def head_kernel(second, row_map, mask, ranks, near, u, v, send, near_buf, u_buf, v_buf, sems):
    row = lax.axis_index("row")
    col = lax.axis_index("col")
    owners = find_owners(row_map)
    panel = 1 if second else jnp.where(row == owners[0] >> 1, 0, 1)
    s = jnp.where(panel == 0, owners[0], owners[1]) & 1
    copies = [
        pltpu.make_async_copy(source.at[s], target, sems.at[i])
        for i, (source, target) in enumerate(((u, u_buf), (v, v_buf), (near, near_buf)))
    ]
    for copy in copies:
        copy.start()
    for copy in copies:
        copy.wait()
    for t in range(2):
        low = low_rank(kept_left(u_buf[t], ranks[s, t]), v_buf[t])
        tile = (near_buf[t].astype(F32) * mask[s, t].astype(F32) + low).astype(BF)
        start = t * WIDE
        send[:, :, start : start + TILE] = tile.reshape(PARTS, CHUNK, TILE)

    @pl.when(col == panel)
    def _():
        tile = near_buf[0] * mask[s, 0].astype(F32).astype(BF)
        factors = lane_blocks(kept_left(u_buf[0], ranks[s, 0]), v_buf[0])
        send[:, :, :TILE] = tile.reshape(PARTS, CHUNK, TILE)
        send[:, :, TILE:WIDE] = factors.reshape(PARTS, CHUNK, LANES)


def head(second, row_map, mask, ranks, near, u, v):
    def kernel(*refs):
        head_kernel(second, *refs)

    return pl.pallas_call(
        kernel,
        out_shape=jax.ShapeDtypeStruct((PARTS, CHUNK, WIDE + TILE), BF),
        in_specs=[SMEM] * 3 + [ANY] * 3,
        out_specs=VMEM,
        scratch_shapes=[
            pltpu.VMEM((2, TILE, TILE), BF),
            pltpu.VMEM((2, KMAX, TILE), BF),
            pltpu.VMEM((2, KMAX, TILE), BF),
            pltpu.SemaphoreType.DMA((3,)),
        ],
        compiler_params=PARAMS,
        name="head_again" if second else "head",
    )(row_map, mask, ranks, near, u, v)


def columns_kernel(mask, ranks, near, u, v, cols):
    for s in range(2):
        cols[s, :, :TILE] = near[s, 0] * mask[s, 0].astype(F32).astype(BF)
        cols[s, :, TILE:] = lane_blocks(kept_left(u[s, 0], ranks[s, 0]), v[s, 0])


def columns(mask, ranks, near, u, v):
    def tiles(height):
        return pl.BlockSpec((2, 1, height, TILE), lambda i: (0, 0, 0, 0))

    return pl.pallas_call(
        columns_kernel,
        grid=(1,),
        out_shape=jax.ShapeDtypeStruct((2, TILE, WIDE), BF),
        in_specs=[SMEM] * 2 + [tiles(TILE), tiles(KMAX), tiles(KMAX)],
        out_specs=pl.BlockSpec((2, TILE, WIDE), lambda i: (0, 0, 0)),
        compiler_params=PARAMS,
        name="columns",
    )(mask, ranks, near, u, v)


def take_kernel(row_map, got0, got1, out, chunk, sems):
    copies = []
    for k, (got, owner) in enumerate(zip((got0, got1), find_owners(row_map))):
        copies.append(pltpu.make_async_copy(got.at[owner >> 1], chunk.at[k], sems.at[k]))
        copies[-1].start()
    for copy in copies:
        copy.wait()
    core = lax.axis_index("col") & 1
    parts = [chunk[0, :, :TILE], chunk[1, :, :TILE], chunk[core, :, TILE:WIDE]]
    parts += [chunk[0, :, WIDE:], chunk[1, :, WIDE:]]
    whole = jnp.concatenate(parts, axis=1)
    for z in range(NZ):
        out[z] = whole


def take(row_map, got0, got1):
    return pl.pallas_call(
        take_kernel,
        out_shape=jax.ShapeDtypeStruct((NZ, CHUNK, FIRST + 2 * TILE), BF),
        in_specs=[SMEM, ANY, ANY],
        out_specs=VMEM,
        scratch_shapes=[pltpu.VMEM((2, CHUNK, WIDE + TILE), BF), pltpu.SemaphoreType.DMA((2,))],
        compiler_params=PARAMS,
        name="take",
    )(row_map, got0, got1)


def fan_kernel(line, pivots, rows0, rows1):
    pivots[...] = line[:, :, :FIRST]
    for y in range(NY):
        rows0[y] = line[:, :, : 2 * TILE]
        rows1[y] = line[:, :, FIRST:]


def fan(line):
    rows = jax.ShapeDtypeStruct((NY, NZ, CHUNK, 2 * TILE), BF)
    return pl.pallas_call(
        fan_kernel,
        out_shape=(jax.ShapeDtypeStruct((NZ, CHUNK, FIRST), BF), rows, rows),
        in_specs=[VMEM],
        out_specs=(VMEM,) * 3,
        compiler_params=PARAMS,
        name="fan",
    )(line)


def fan_pivots_kernel(own, hop1, hop3, hop2, out):
    x = lax.axis_index("col") >> 1

    @pl.when(x == 0)
    def _():
        for y in range(NY):
            out[y] = own[...]

    @pl.when(x != 0)
    def _():
        pivots = hop1[...] + hop3[...] + hop2[...]
        for y in range(NY):
            out[y] = pivots


def fan_pivots(own, hops):
    return pl.pallas_call(
        fan_pivots_kernel,
        out_shape=jax.ShapeDtypeStruct((NY, NZ, CHUNK, FIRST), BF),
        in_specs=[VMEM] * 4,
        out_specs=VMEM,
        compiler_params=PARAMS,
        name="fan_pivots",
    )(own, *hops)


def chain_kernel(own, other, out, piv):
    core = lax.axis_index("col") & 1
    piv[core] = own[...].reshape(TILE, FIRST)
    piv[1 - core] = other[...].reshape(TILE, FIRST)
    inv0 = inverse(build(piv[0, :, :TILE], piv[0, :, 2 * TILE :], True))
    row1 = piv[1, :, :TILE]
    mult_p1 = dot(piv[0, :, TILE : 2 * TILE], inv0).astype(BF)
    out[0] = inv0
    out[1] = row1
    out[2] = mult_p1
    pivot = build(piv[1, :, TILE : 2 * TILE], piv[1, :, 2 * TILE :], True)
    out[3] = inverse(pivot - dot(mult_p1, row1))


def chain(own, other):
    return pl.pallas_call(
        chain_kernel,
        out_shape=jax.ShapeDtypeStruct((4, TILE, TILE), BF),
        in_specs=[VMEM] * 2,
        out_specs=VMEM,
        scratch_shapes=[pltpu.VMEM((2, TILE, FIRST), BF)],
        compiler_params=PARAMS,
        cost_estimate=pl.CostEstimate(flops=28 * 2 * TILE**3, bytes_accessed=5 << 20, transcendentals=0),
        name="chain",
    )(own, other)


def own_kernel(row_map, mask, ranks, near, u, v, out):
    row = lax.axis_index("row")
    col = lax.axis_index("col")
    t = pl.program_id(1)
    s = pl.program_id(0)
    tile = near[0, 0].astype(F32) * mask[s, t].astype(F32)
    out[0, 0] = tile + low_rank(kept_left(u[0, 0], ranks[s, t]), v[0, 0])

    @pl.when(row_map[2 * row + s] == t * 2 * NX + col)
    def _():
        out[0, 0] += SHIFT * eye()


def own_tiles(row_map, mask, ranks, near, u, v):
    def tiles(height):
        return pl.BlockSpec((1, 1, height, TILE), lambda s, t: (s, t, 0, 0))

    return pl.pallas_call(
        own_kernel,
        grid=(2, 2),
        out_shape=jax.ShapeDtypeStruct((2, 2, TILE, TILE), F32),
        in_specs=[SMEM] * 3 + [tiles(TILE), tiles(KMAX), tiles(KMAX)],
        out_specs=tiles(TILE),
        compiler_params=SMALL,
        cost_estimate=pl.CostEstimate(flops=4 * 2 * TILE**3, bytes_accessed=7 << 20, transcendentals=0),
        name="own_tiles",
    )(row_map, mask, ranks, near, u, v)


def columns_built_kernel(row_map, own, other, first, second, cols):
    core = lax.axis_index("col") & 1
    row = lax.axis_index("row")
    cols[core] = own[...]
    cols[1 - core] = other[...]
    for s in range(2):
        held = row_map[2 * row + s]
        first[s] = build(cols[0, s, :, :TILE], cols[0, s, :, TILE:], held == 0).astype(BF)
        second[s] = build(cols[1, s, :, :TILE], cols[1, s, :, TILE:], held == 1)


def columns_built(row_map, own, other):
    return pl.pallas_call(
        columns_built_kernel,
        out_shape=(
            jax.ShapeDtypeStruct((2, TILE, TILE), BF),
            jax.ShapeDtypeStruct((2, TILE, TILE), F32),
        ),
        in_specs=[SMEM] + [VMEM] * 2,
        out_specs=(VMEM, VMEM),
        scratch_shapes=[pltpu.VMEM((2, 2, TILE, WIDE), BF)],
        compiler_params=SMALL,
        cost_estimate=pl.CostEstimate(flops=4 * 2 * TILE**3, bytes_accessed=6 << 20, transcendentals=0),
        name="columns_built",
    )(row_map, own, other)


def mults_kernel(row_map, first, second, lead, out):
    row = lax.axis_index("row")
    for s in range(2):
        held = row_map[2 * row + s]
        mult = jnp.where(held > 0, dot(first[s], lead[0]), 0.0).astype(BF)
        out[s, :, :TILE] = mult
        tile = second[s] - dot(mult, lead[1])
        out[s, :, TILE:] = jnp.where(held > 1, dot(tile.astype(BF), lead[3]), 0.0).astype(BF)


def mults(row_map, first, second, lead):
    return pl.pallas_call(
        mults_kernel,
        out_shape=jax.ShapeDtypeStruct((2, TILE, 2 * TILE), BF),
        in_specs=[SMEM] + [VMEM] * 3,
        out_specs=VMEM,
        compiler_params=SMALL,
        cost_estimate=pl.CostEstimate(flops=6 * 2 * TILE**3, bytes_accessed=7 << 20, transcendentals=0),
        name="mults",
    )(row_map, first, second, lead)


def last_kernel(rows0, rows1, own, lead, mult, out, rows_buf, pivot_rows, out_buf, sems, out_sems):
    col = lax.axis_index("col")
    copies = {
        t: pltpu.make_async_copy(source, rows_buf.at[t], sems.at[t]) for t, source in ((1, rows1), (0, rows0))
    }
    for copy in copies.values():
        copy.start()
    stores = []
    for t in (1, 0):
        j = t * 2 * NX + col
        copies[t].wait()
        row0 = rows_buf[t, :, :, :, :TILE].reshape(TILE, TILE)
        if t == 0:
            row0 = jnp.where(j == 1, lead[1].astype(F32), row0.astype(F32))
            row0 = jnp.where(j > 0, row0, 0.0).astype(BF)
        row1 = rows_buf[t, :, :, :, TILE:].reshape(TILE, TILE).astype(F32) - dot(lead[2], row0)
        if t == 0:
            row1 = jnp.where(j > 1, row1, 0.0)
        pivot_rows[t, :TILE] = row0
        pivot_rows[t, TILE:] = row1.astype(BF)
        for s in range(2):
            out_buf[s, t] = (own[s, t] - dot(mult[s], pivot_rows[t])).astype(BF)
            stores.append(pltpu.make_async_copy(out_buf.at[s, t], out.at[s, t], out_sems.at[s, t]))
            stores[-1].start()
    for store in stores:
        store.wait()


def last(rows0, rows1, own, lead, mult):
    return pl.pallas_call(
        last_kernel,
        out_shape=jax.ShapeDtypeStruct((2, 2, TILE, TILE), BF),
        in_specs=[ANY] * 2 + [VMEM] * 3,
        out_specs=ANY,
        scratch_shapes=[
            pltpu.VMEM((2, NY, NZ, CHUNK, 2 * TILE), BF),
            pltpu.VMEM((2, 2 * TILE, TILE), BF),
            pltpu.VMEM((2, 2, TILE, TILE), BF),
            pltpu.SemaphoreType.DMA((2,)),
            pltpu.SemaphoreType.DMA((2, 2)),
        ],
        compiler_params=SMALL,
        cost_estimate=pl.CostEstimate(flops=12 * 2 * TILE**3, bytes_accessed=10 << 20, transcendentals=0),
        name="last",
    )(rows0, rows1, own, lead, mult)


def pairs(source, target):
    return [(source * 2 + core, target * 2 + core) for core in range(2)]


def body(near_tiles, basis_u, basis_v, near_mask, ranks, row_map):
    near = near_tiles.reshape(2, 2, TILE, TILE)
    u = basis_u.reshape(2, 2, KMAX, TILE)
    v = basis_v.reshape(2, 2, KMAX, TILE)
    mask = near_mask.reshape(2, 2)
    ranks = ranks.reshape(2, 2)
    x = lax.axis_index("col") >> 1

    send = head(False, row_map, mask, ranks, near, u, v)

    def scatter(part):
        return lax.all_to_all(part, "row", 0, 0)

    def first_hop():
        cols = columns(mask, ranks, near, u, v)
        return [cols] + [lax.ppermute(cols, "col", pairs(0, to)) for to in (1, 3)]

    def apart():
        again = head(True, row_map, mask, ranks, near, u, v)
        got = [scatter(send), scatter(again)]
        return take(row_map, *got), first_hop()

    def merged():
        got = scatter(send)
        return take(row_map, got, got), first_hop()

    device = jnp.arange(NROWS, dtype=jnp.int32) >> 1
    apart_by = jnp.sum(jnp.where(row_map == 0, device, 0) - jnp.where(row_map == 1, device, 0))
    one_device = apart_by == 0
    line, hop = lax.cond(one_device, apart, merged)

    cols = jnp.where(x == 0, hop[0], hop[1] + hop[2])
    hop = [lax.ppermute(cols[s], "col", pairs(source, 2)) for s, source in enumerate((1, 3))]
    cols = jnp.where(x == 2, jnp.stack(hop), cols)
    swap = [(c, c ^ 1) for c in range(2 * NX)]

    z_groups = [[y * NZ + z for z in range(NZ)] for y in range(NY)]
    y_groups = [[y * NZ + z for y in range(NY)] for z in range(NZ)]
    line, near, u, v = lax.optimization_barrier((line, near, u, v))
    line = lax.all_to_all(line, "row", 0, 0, axis_index_groups=z_groups)
    own = own_tiles(row_map, mask, ranks, near, u, v)

    def gather(part):
        return lax.all_to_all(part, "row", 0, 0, axis_index_groups=y_groups)

    pivots, rows0, rows1 = fan(line)
    rows1 = gather(rows1)
    hops = [lax.ppermute(pivots, "col", pairs(0, to)) for to in (1, 3, 2)]
    hops, rows1 = lax.optimization_barrier((hops, rows1))
    piv = gather(fan_pivots(pivots, hops))
    rows0, piv = lax.optimization_barrier((rows0, piv))
    rows0 = gather(rows0)
    lead = chain(piv, lax.ppermute(piv, "col", swap))
    first, second = columns_built(row_map, cols, lax.ppermute(cols, "col", swap))
    mult = mults(row_map, first, second, lead)
    out = last(rows0, rows1, own, lead, mult)
    return out.reshape(2, 2, 1, TILE, TILE)


def solution(mesh):
    return jax.shard_map(
        body,
        mesh=mesh,
        in_specs=(
            P("row", None, "col", None, None),
            P("row", None, "col", None, None),
            P("row", None, "col", None, None),
            P("row", None, "col"),
            P("row", None, "col"),
            P(),
        ),
        out_specs=P("row", None, "col", None, None),
        check_vma=False,
    )
```

```python
import math

import jax
import jax.numpy as jnp
from jax import lax
from jax.experimental import pallas as pl
from jax.experimental.pallas import tpu as pltpu
from jax.sharding import PartitionSpec as P

TILE = 512
KMAX = 64
LANES = 128
WIDE = TILE + LANES
FIRST = TILE + WIDE
BLOCKS = TILE // LANES
CHUNK = 16
PARTS = TILE // CHUNK
NROWS = 64
SHIFT = 1.1 * math.sqrt(TILE)
NY, NZ, NX = 4, 8, 4
BF = jnp.bfloat16
F32 = jnp.float32

SMEM = pl.BlockSpec(memory_space=pltpu.SMEM)
VMEM = pl.BlockSpec(memory_space=pltpu.VMEM)
ANY = pl.BlockSpec(memory_space=pl.ANY)
PARAMS = pltpu.CompilerParams(vmem_limit_bytes=32 << 20)
SMALL = pltpu.CompilerParams(vmem_limit_bytes=28 << 20)


def dot(a, b):
    return jnp.dot(a, b, preferred_element_type=F32)


def split(a):
    high = a.astype(BF)
    return high, (a - high.astype(F32)).astype(BF)


def dot_hi(a, b):
    return dot(a[0], b[0]) + (dot(a[0], b[1]) + dot(a[1], b[0]))


def eye():
    rows = lax.broadcasted_iota(jnp.int32, (TILE, TILE), 0)
    cols = lax.broadcasted_iota(jnp.int32, (TILE, TILE), 1)
    return (rows == cols).astype(F32)


def low_rank(left, right):
    return lax.dot_general(left, right, (((0,), (0,)), ((), ())), preferred_element_type=F32)


def build(near, factors, diag):
    factors = factors.reshape(BLOCKS, 2, KMAX, LANES)
    left = jnp.concatenate([factors[k, 0] for k in range(BLOCKS)], axis=1)
    right = jnp.concatenate([factors[k, 1] for k in range(BLOCKS)], axis=1)
    tile = near.astype(F32) + low_rank(left, right)
    return tile + jnp.where(diag, SHIFT, 0.0) * eye()


def inverse(pivot):
    ident = eye()
    e = ident - pivot * (1.0 / SHIFT)
    es = split(e)
    e2 = dot_hi(es, es)
    e2s = split(e2)
    total = split(ident + e + e2 + dot_hi(es, e2s))
    e4 = dot_hi(e2s, e2s)
    whole = total[0].astype(F32) + total[1].astype(F32) + dot_hi(total, split(e4))
    return (whole * (1.0 / SHIFT)).astype(BF)


def kept_left(u, rank):
    rows = lax.broadcasted_iota(jnp.int32, (KMAX, TILE), 0)
    return jnp.where(rows < rank, u.astype(F32), 0.0).astype(BF)


def lane_blocks(left, right):
    parts = []
    for k in range(BLOCKS):
        cut = slice(k * LANES, (k + 1) * LANES)
        parts += [left[:, cut], right[:, cut]]
    return jnp.concatenate(parts, axis=0)


def find_owners(row_map):
    def step(slot, found):
        held = row_map[slot]
        return jnp.where(held == 0, slot, found[0]), jnp.where(held == 1, slot, found[1])

    return lax.fori_loop(0, NROWS, step, (0, 0), unroll=8)


def head_kernel(second, row_map, mask, ranks, near, u, v, send, near_buf, u_buf, v_buf, sems):
    row = lax.axis_index("row")
    col = lax.axis_index("col")
    owners = find_owners(row_map)
    panel = 1 if second else jnp.where(row == owners[0] >> 1, 0, 1)
    s = jnp.where(panel == 0, owners[0], owners[1]) & 1
    copies = [
        pltpu.make_async_copy(source.at[s], target, sems.at[i])
        for i, (source, target) in enumerate(((u, u_buf), (v, v_buf), (near, near_buf)))
    ]
    for copy in copies:
        copy.start()
    for copy in copies:
        copy.wait()
    for t in range(2):
        low = low_rank(kept_left(u_buf[t], ranks[s, t]), v_buf[t])
        tile = (near_buf[t].astype(F32) * mask[s, t].astype(F32) + low).astype(BF)
        start = t * WIDE
        send[:, :, start : start + TILE] = tile.reshape(PARTS, CHUNK, TILE)

    @pl.when(col == panel)
    def _():
        tile = near_buf[0] * mask[s, 0].astype(F32).astype(BF)
        factors = lane_blocks(kept_left(u_buf[0], ranks[s, 0]), v_buf[0])
        send[:, :, :TILE] = tile.reshape(PARTS, CHUNK, TILE)
        send[:, :, TILE:WIDE] = factors.reshape(PARTS, CHUNK, LANES)


def head(second, row_map, mask, ranks, near, u, v):
    def kernel(*refs):
        head_kernel(second, *refs)

    return pl.pallas_call(
        kernel,
        out_shape=jax.ShapeDtypeStruct((PARTS, CHUNK, WIDE + TILE), BF),
        in_specs=[SMEM] * 3 + [ANY] * 3,
        out_specs=VMEM,
        scratch_shapes=[
            pltpu.VMEM((2, TILE, TILE), BF),
            pltpu.VMEM((2, KMAX, TILE), BF),
            pltpu.VMEM((2, KMAX, TILE), BF),
            pltpu.SemaphoreType.DMA((3,)),
        ],
        compiler_params=PARAMS,
        name="head_again" if second else "head",
    )(row_map, mask, ranks, near, u, v)


def columns_kernel(row_map, mask, ranks, near, u, v, cols):
    row = lax.axis_index("row")
    col = lax.axis_index("col")
    for s in range(2):
        tile = near[s, 0].astype(F32) * mask[s, 0].astype(F32)
        tile = tile + low_rank(kept_left(u[s, 0], ranks[s, 0]), v[s, 0])
        tile = tile + jnp.where(row_map[2 * row + s] == col, SHIFT, 0.0) * eye()
        cols[s] = tile.astype(BF)


def columns(row_map, mask, ranks, near, u, v):
    def tiles(height):
        return pl.BlockSpec((2, 1, height, TILE), lambda i: (0, 0, 0, 0))

    return pl.pallas_call(
        columns_kernel,
        grid=(1,),
        out_shape=jax.ShapeDtypeStruct((2, TILE, TILE), BF),
        in_specs=[SMEM] * 3 + [tiles(TILE), tiles(KMAX), tiles(KMAX)],
        out_specs=pl.BlockSpec((2, TILE, TILE), lambda i: (0, 0, 0)),
        compiler_params=PARAMS,
        name="columns",
    )(row_map, mask, ranks, near, u, v)


def take_kernel(row_map, got0, got1, out, chunk, sems):
    copies = []
    for k, (got, owner) in enumerate(zip((got0, got1), find_owners(row_map))):
        copies.append(pltpu.make_async_copy(got.at[owner >> 1], chunk.at[k], sems.at[k]))
        copies[-1].start()
    for copy in copies:
        copy.wait()
    core = lax.axis_index("col") & 1
    parts = [chunk[0, :, :TILE], chunk[1, :, :TILE], chunk[core, :, TILE:WIDE]]
    parts += [chunk[0, :, WIDE:], chunk[1, :, WIDE:]]
    whole = jnp.concatenate(parts, axis=1)
    for z in range(NZ):
        out[z] = whole


def take(row_map, got0, got1):
    return pl.pallas_call(
        take_kernel,
        out_shape=jax.ShapeDtypeStruct((NZ, CHUNK, FIRST + 2 * TILE), BF),
        in_specs=[SMEM, ANY, ANY],
        out_specs=VMEM,
        scratch_shapes=[pltpu.VMEM((2, CHUNK, WIDE + TILE), BF), pltpu.SemaphoreType.DMA((2,))],
        compiler_params=PARAMS,
        name="take",
    )(row_map, got0, got1)


def fan_kernel(line, pivots, rows0, rows1):
    pivots[...] = line[:, :, :FIRST]
    for y in range(NY):
        rows0[y] = line[:, :, : 2 * TILE]
        rows1[y] = line[:, :, FIRST:]


def fan(line):
    rows = jax.ShapeDtypeStruct((NY, NZ, CHUNK, 2 * TILE), BF)
    return pl.pallas_call(
        fan_kernel,
        out_shape=(jax.ShapeDtypeStruct((NZ, CHUNK, FIRST), BF), rows, rows),
        in_specs=[VMEM],
        out_specs=(VMEM,) * 3,
        compiler_params=PARAMS,
        name="fan",
    )(line)


def fan_pivots_kernel(own, hop1, hop3, hop2, out):
    x = lax.axis_index("col") >> 1

    @pl.when(x == 0)
    def _():
        for y in range(NY):
            out[y] = own[...]

    @pl.when(x != 0)
    def _():
        pivots = hop1[...] + hop3[...] + hop2[...]
        for y in range(NY):
            out[y] = pivots


def fan_pivots(own, hops):
    return pl.pallas_call(
        fan_pivots_kernel,
        out_shape=jax.ShapeDtypeStruct((NY, NZ, CHUNK, FIRST), BF),
        in_specs=[VMEM] * 4,
        out_specs=VMEM,
        compiler_params=PARAMS,
        name="fan_pivots",
    )(own, *hops)


def own_kernel(row_map, mask, ranks, near, u, v, out):
    row = lax.axis_index("row")
    col = lax.axis_index("col")
    t = pl.program_id(1)
    s = pl.program_id(0)
    tile = near[0, 0].astype(F32) * mask[s, t].astype(F32)
    out[0, 0] = tile + low_rank(kept_left(u[0, 0], ranks[s, t]), v[0, 0])

    @pl.when(row_map[2 * row + s] == t * 2 * NX + col)
    def _():
        out[0, 0] += SHIFT * eye()


def own_tiles(row_map, mask, ranks, near, u, v):
    def tiles(height):
        return pl.BlockSpec((1, 1, height, TILE), lambda s, t: (s, t, 0, 0))

    return pl.pallas_call(
        own_kernel,
        grid=(2, 2),
        out_shape=jax.ShapeDtypeStruct((2, 2, TILE, TILE), F32),
        in_specs=[SMEM] * 3 + [tiles(TILE), tiles(KMAX), tiles(KMAX)],
        out_specs=tiles(TILE),
        compiler_params=SMALL,
        cost_estimate=pl.CostEstimate(flops=4 * 2 * TILE**3, bytes_accessed=7 << 20, transcendentals=0),
        name="own_tiles",
    )(row_map, mask, ranks, near, u, v)


def panel_kernel(
    row_map, piv_own, piv_other, cols_own, cols_other, rows1, own, lead, mult, out,
    piv, cols, rows, tiles, pivot_rows, out_buf, sems, out_sems,
):
    core = lax.axis_index("col") & 1
    row = lax.axis_index("row")
    moves = (
        (piv_own, piv.at[core]),
        (piv_other, piv.at[1 - core]),
        (cols_own, cols.at[core]),
        (cols_other, cols.at[1 - core]),
        (rows1, rows),
        (own.at[:, 1], tiles),
    )
    copies = [pltpu.make_async_copy(*move, sems.at[i]) for i, move in enumerate(moves)]
    for copy in copies:
        copy.start()
    copies[0].wait()
    copies[1].wait()

    def part(j, lanes):
        return piv[j, :, :, :, lanes].reshape(TILE, -1)

    firsts = slice(0, TILE)
    seconds = slice(TILE, 2 * TILE)
    factors = slice(2 * TILE, FIRST)
    inv0 = inverse(build(part(0, firsts), part(0, factors), True))
    row1 = part(1, firsts)
    lead[0] = row1
    mult_p1 = dot(part(0, seconds), inv0).astype(BF)
    lead[1] = mult_p1
    inv1 = inverse(build(part(1, seconds), part(1, factors), True) - dot(mult_p1, row1))
    copies[2].wait()
    copies[3].wait()
    for s in range(2):
        held = row_map[2 * row + s]
        first = jnp.where(held > 0, dot(cols[0, s], inv0), 0.0).astype(BF)
        second = cols[1, s].astype(F32) - dot(first, row1)
        mult[s, :, :TILE] = first
        mult[s, :, TILE:] = jnp.where(held > 1, dot(second.astype(BF), inv1), 0.0).astype(BF)
    copies[4].wait()
    copies[5].wait()
    update(rows[..., :TILE].reshape(TILE, TILE), rows, lead, mult, tiles, pivot_rows, out, out_buf, out_sems, 1)


def update(row0, rows, lead, mult, tiles, pivot_rows, out, out_buf, out_sems, t):
    row1 = rows[..., TILE:].reshape(TILE, TILE).astype(F32) - dot(lead[1], row0)
    if t == 0:
        row1 = jnp.where(lax.axis_index("col") > 1, row1, 0.0)
    pivot_rows[:TILE] = row0
    pivot_rows[TILE:] = row1.astype(BF)
    stores = []
    for s in range(2):
        out_buf[s] = (tiles[s] - dot(mult[s], pivot_rows[...])).astype(BF)
        stores.append(pltpu.make_async_copy(out_buf.at[s], out.at[s, t], out_sems.at[s]))
        stores[-1].start()
    for store in stores:
        store.wait()


def panel(row_map, piv_own, piv_other, cols_own, cols_other, rows1, own):
    return pl.pallas_call(
        panel_kernel,
        out_shape=(
            jax.ShapeDtypeStruct((2, TILE, TILE), BF),
            jax.ShapeDtypeStruct((2, TILE, 2 * TILE), BF),
            jax.ShapeDtypeStruct((2, 2, TILE, TILE), BF),
        ),
        in_specs=[SMEM] + [ANY] * 6,
        out_specs=(VMEM, VMEM, ANY),
        scratch_shapes=[
            pltpu.VMEM((2, NY, NZ, CHUNK, FIRST), BF),
            pltpu.VMEM((2, 2, TILE, TILE), BF),
            pltpu.VMEM((NY, NZ, CHUNK, 2 * TILE), BF),
            pltpu.VMEM((2, TILE, TILE), F32),
            pltpu.VMEM((2 * TILE, TILE), BF),
            pltpu.VMEM((2, TILE, TILE), BF),
            pltpu.SemaphoreType.DMA((6,)),
            pltpu.SemaphoreType.DMA((2,)),
        ],
        compiler_params=PARAMS,
        cost_estimate=pl.CostEstimate(flops=38 * 2 * TILE**3, bytes_accessed=5 << 20, transcendentals=0),
        name="panel",
    )(row_map, piv_own, piv_other, cols_own, cols_other, rows1, own)


def last_kernel(rows0, own, lead, mult, begun, out, rows, tiles, pivot_rows, out_buf, sems, out_sems):
    del begun
    col = lax.axis_index("col")
    copies = [
        pltpu.make_async_copy(rows0, rows, sems.at[0]),
        pltpu.make_async_copy(own.at[:, 0], tiles, sems.at[1]),
    ]
    for copy in copies:
        copy.start()
    for copy in copies:
        copy.wait()
    row0 = rows[..., :TILE].reshape(TILE, TILE).astype(F32)
    row0 = jnp.where(col == 1, lead[0].astype(F32), row0)
    row0 = jnp.where(col > 0, row0, 0.0).astype(BF)
    update(row0, rows, lead, mult, tiles, pivot_rows, out, out_buf, out_sems, 0)


def last(rows0, own, lead, mult, begun):
    return pl.pallas_call(
        last_kernel,
        out_shape=jax.ShapeDtypeStruct((2, 2, TILE, TILE), BF),
        in_specs=[ANY] * 2 + [VMEM] * 2 + [ANY],
        out_specs=ANY,
        input_output_aliases={4: 0},
        scratch_shapes=[
            pltpu.VMEM((NY, NZ, CHUNK, 2 * TILE), BF),
            pltpu.VMEM((2, TILE, TILE), F32),
            pltpu.VMEM((2 * TILE, TILE), BF),
            pltpu.VMEM((2, TILE, TILE), BF),
            pltpu.SemaphoreType.DMA((2,)),
            pltpu.SemaphoreType.DMA((2,)),
        ],
        compiler_params=SMALL,
        cost_estimate=pl.CostEstimate(flops=6 * 2 * TILE**3, bytes_accessed=6 << 20, transcendentals=0),
        name="last",
    )(rows0, own, lead, mult, begun)


def pairs(source, target):
    return [(source * 2 + core, target * 2 + core) for core in range(2)]


def body(near_tiles, basis_u, basis_v, near_mask, ranks, row_map):
    near = near_tiles.reshape(2, 2, TILE, TILE)
    u = basis_u.reshape(2, 2, KMAX, TILE)
    v = basis_v.reshape(2, 2, KMAX, TILE)
    mask = near_mask.reshape(2, 2)
    ranks = ranks.reshape(2, 2)
    x = lax.axis_index("col") >> 1

    send = head(False, row_map, mask, ranks, near, u, v)

    def scatter(part):
        return lax.all_to_all(part, "row", 0, 0)

    def beside():
        cols = columns(row_map, mask, ranks, near, u, v)
        hop = [lax.ppermute(cols, "col", pairs(0, to)) for to in (1, 3)]
        return cols, hop, own_tiles(row_map, mask, ranks, near, u, v)

    def apart():
        again = head(True, row_map, mask, ranks, near, u, v)
        got = [scatter(send), scatter(again)]
        return take(row_map, *got), beside()

    def merged():
        got = scatter(send)
        return take(row_map, got, got), beside()

    device = jnp.arange(NROWS, dtype=jnp.int32) >> 1
    apart_by = jnp.sum(jnp.where(row_map == 0, device, 0) - jnp.where(row_map == 1, device, 0))
    one_device = apart_by == 0
    line, (cols, hop, own) = lax.cond(one_device, apart, merged)

    cols = jnp.where(x == 0, cols, hop[0] + hop[1])
    hop = [lax.ppermute(cols[s], "col", pairs(source, 2)) for s, source in enumerate((1, 3))]
    cols = jnp.where(x == 2, jnp.stack(hop), cols)
    swap = [(c, c ^ 1) for c in range(2 * NX)]

    z_groups = [[y * NZ + z for z in range(NZ)] for y in range(NY)]
    y_groups = [[y * NZ + z for y in range(NY)] for z in range(NZ)]
    line = lax.all_to_all(line, "row", 0, 0, axis_index_groups=z_groups)

    def gather(part):
        return lax.all_to_all(part, "row", 0, 0, axis_index_groups=y_groups)

    pivots, rows0, rows1 = fan(line)
    rows1 = gather(rows1)
    hops = [lax.ppermute(pivots, "col", pairs(0, to)) for to in (1, 3, 2)]
    hops, rows1 = lax.optimization_barrier((hops, rows1))
    piv = gather(fan_pivots(pivots, hops))
    rows0, piv = lax.optimization_barrier((rows0, piv))
    rows0 = gather(rows0)
    piv_other = lax.ppermute(piv, "col", swap)
    cols_other = lax.ppermute(cols, "col", swap)
    lead, mult, begun = panel(row_map, piv, piv_other, cols, cols_other, rows1, own)
    out = last(rows0, own, lead, mult, begun)
    return out.reshape(2, 2, 1, TILE, TILE)


def solution(mesh):
    return jax.shard_map(
        body,
        mesh=mesh,
        in_specs=(
            P("row", None, "col", None, None),
            P("row", None, "col", None, None),
            P("row", None, "col", None, None),
            P("row", None, "col"),
            P("row", None, "col"),
            P(),
        ),
        out_specs=P("row", None, "col", None, None),
        check_vma=False,
    )
```

```python
import math

import jax
import jax.numpy as jnp
from jax import lax
from jax.experimental import pallas as pl
from jax.experimental.pallas import tpu as pltpu
from jax.sharding import PartitionSpec as P

TILE = 512
KMAX = 64
LANES = 128
WIDE = TILE + LANES
FIRST = TILE + WIDE
BLOCKS = TILE // LANES
CHUNK = 16
PARTS = TILE // CHUNK
NROWS = 64
SHIFT = 1.1 * math.sqrt(TILE)
NY, NZ, NX = 4, 8, 4
BF = jnp.bfloat16
F32 = jnp.float32

SMEM = pl.BlockSpec(memory_space=pltpu.SMEM)
VMEM = pl.BlockSpec(memory_space=pltpu.VMEM)
ANY = pl.BlockSpec(memory_space=pl.ANY)


def grant(mib):
    return pltpu.CompilerParams(vmem_limit_bytes=mib << 20)


def in_hbm(shape, dtype=BF):
    return pltpu.HBM(shape, dtype)


def pin(space, *arrays):
    return [pltpu.with_memory_space_constraint(array, space) for array in arrays]


def dot(a, b):
    return jnp.dot(a, b, preferred_element_type=F32)


def split(a):
    high = a.astype(BF)
    return high, (a - high.astype(F32)).astype(BF)


def dot_hi(a, b):
    left = jnp.concatenate([a[0], a[0], a[1]], axis=1)
    return dot(left, jnp.concatenate([b[0], b[1], b[0]], axis=0))


def eye():
    rows = lax.broadcasted_iota(jnp.int32, (TILE, TILE), 0)
    cols = lax.broadcasted_iota(jnp.int32, (TILE, TILE), 1)
    return (rows == cols).astype(F32)


def low_rank(left, right):
    return lax.dot_general(left, right, (((0,), (0,)), ((), ())), preferred_element_type=F32)


def build(near, factors, diag):
    factors = factors.reshape(BLOCKS, 2, KMAX, LANES)
    left = jnp.concatenate([factors[k, 0] for k in range(BLOCKS)], axis=1)
    right = jnp.concatenate([factors[k, 1] for k in range(BLOCKS)], axis=1)
    tile = near.astype(F32) + low_rank(left, right)
    return tile + jnp.where(diag, SHIFT, 0.0) * eye()


def inverse(pivot):
    ident = eye()
    e = ident - pivot * (1.0 / SHIFT)
    es = split(e)
    e2 = dot_hi(es, es)
    e2s = split(e2)
    total = split(ident + e + e2 + dot_hi(es, e2s))
    e4 = dot_hi(e2s, e2s)
    whole = total[0].astype(F32) + total[1].astype(F32) + dot_hi(total, split(e4))
    return (whole * (1.0 / SHIFT)).astype(BF)


def kept_left(u, rank):
    rows = lax.broadcasted_iota(jnp.int32, (KMAX, TILE), 0)
    return jnp.where(rows < rank, u.astype(F32), 0.0).astype(BF)


def lane_blocks(left, right):
    parts = []
    for k in range(BLOCKS):
        cut = slice(k * LANES, (k + 1) * LANES)
        parts += [left[:, cut], right[:, cut]]
    return jnp.concatenate(parts, axis=0)


def find_owners(row_map):
    def step(slot, found):
        held = row_map[slot]
        return jnp.where(held == 0, slot, found[0]), jnp.where(held == 1, slot, found[1])

    return lax.fori_loop(0, NROWS, step, (0, 0), unroll=8)


def head_kernel(second, row_map, mask, ranks, near, u, v, send, near_buf, u_buf, v_buf, sems):
    row = lax.axis_index("row")
    col = lax.axis_index("col")
    owners = find_owners(row_map)
    panel = 1 if second else jnp.where(row == owners[0] >> 1, 0, 1)
    s = jnp.where(panel == 0, owners[0], owners[1]) & 1
    copies = [
        pltpu.make_async_copy(source.at[s], target, sems.at[i])
        for i, (source, target) in enumerate(((u, u_buf), (v, v_buf), (near, near_buf)))
    ]
    for copy in copies:
        copy.start()
    for copy in copies:
        copy.wait()
    for t in range(2):
        low = low_rank(kept_left(u_buf[t], ranks[s, t]), v_buf[t])
        tile = (near_buf[t].astype(F32) * mask[s, t].astype(F32) + low).astype(BF)
        start = t * WIDE
        send[:, :, start : start + TILE] = tile.reshape(PARTS, CHUNK, TILE)

    @pl.when(col == panel)
    def _():
        tile = near_buf[0] * mask[s, 0].astype(F32).astype(BF)
        factors = lane_blocks(kept_left(u_buf[0], ranks[s, 0]), v_buf[0])
        send[:, :, :TILE] = tile.reshape(PARTS, CHUNK, TILE)
        send[:, :, TILE:WIDE] = factors.reshape(PARTS, CHUNK, LANES)


def head(second, row_map, mask, ranks, near, u, v):
    def kernel(*refs):
        head_kernel(second, *refs)

    return pl.pallas_call(
        kernel,
        out_shape=in_hbm((PARTS, CHUNK, WIDE + TILE)),
        in_specs=[SMEM] * 3 + [ANY] * 3,
        out_specs=VMEM,
        scratch_shapes=[
            pltpu.VMEM((2, TILE, TILE), BF),
            pltpu.VMEM((2, KMAX, TILE), BF),
            pltpu.VMEM((2, KMAX, TILE), BF),
            pltpu.SemaphoreType.DMA((3,)),
        ],
        compiler_params=grant(12),
        name="head_again" if second else "head",
    )(row_map, mask, ranks, near, u, v)


def columns_kernel(row_map, mask, ranks, near, u, v, cols):
    row = lax.axis_index("row")
    col = lax.axis_index("col")
    for s in range(2):
        tile = near[s, 0].astype(F32) * mask[s, 0].astype(F32)
        tile = tile + low_rank(kept_left(u[s, 0], ranks[s, 0]), v[s, 0])
        tile = tile + jnp.where(row_map[2 * row + s] == col, SHIFT, 0.0) * eye()
        cols[s] = tile.astype(BF)


def columns(row_map, mask, ranks, near, u, v):
    def tiles(height):
        return pl.BlockSpec((2, 1, height, TILE), lambda i: (0, 0, 0, 0))

    return pl.pallas_call(
        columns_kernel,
        grid=(1,),
        out_shape=in_hbm((2, TILE, TILE)),
        in_specs=[SMEM] * 3 + [tiles(TILE), tiles(KMAX), tiles(KMAX)],
        out_specs=pl.BlockSpec((2, TILE, TILE), lambda i: (0, 0, 0)),
        compiler_params=grant(10),
        name="columns",
    )(row_map, mask, ranks, near, u, v)


def take_kernel(row_map, got0, got1, out, chunk, sems):
    copies = []
    for k, (got, owner) in enumerate(zip((got0, got1), find_owners(row_map))):
        copies.append(pltpu.make_async_copy(got.at[owner >> 1], chunk.at[k], sems.at[k]))
        copies[-1].start()
    for copy in copies:
        copy.wait()
    core = lax.axis_index("col") & 1
    parts = [chunk[0, :, :TILE], chunk[1, :, :TILE], chunk[core, :, TILE:WIDE]]
    parts += [chunk[0, :, WIDE:], chunk[1, :, WIDE:]]
    whole = jnp.concatenate(parts, axis=1)
    for z in range(NZ):
        out[z] = whole


def take(row_map, got0, got1):
    return pl.pallas_call(
        take_kernel,
        out_shape=in_hbm((NZ, CHUNK, FIRST + 2 * TILE)),
        in_specs=[SMEM, ANY, ANY],
        out_specs=VMEM,
        scratch_shapes=[pltpu.VMEM((2, CHUNK, WIDE + TILE), BF), pltpu.SemaphoreType.DMA((2,))],
        compiler_params=grant(8),
        name="take",
    )(row_map, got0, got1)


def fan_kernel(line, pivots, rows0, rows1):
    pivots[...] = line[:, :, :FIRST]
    for y in range(NY):
        rows0[y] = line[:, :, : 2 * TILE]
        rows1[y] = line[:, :, FIRST:]


def fan(line):
    rows = in_hbm((NY, NZ, CHUNK, 2 * TILE))
    return pl.pallas_call(
        fan_kernel,
        out_shape=(jax.ShapeDtypeStruct((NZ, CHUNK, FIRST), BF), rows, rows),
        in_specs=[VMEM],
        out_specs=(VMEM,) * 3,
        compiler_params=grant(8),
        name="fan",
    )(line)


def fan_pivots_kernel(own, hop1, hop3, hop2, out):
    x = lax.axis_index("col") >> 1

    @pl.when(x == 0)
    def _():
        for y in range(NY):
            out[y] = own[...]

    @pl.when(x != 0)
    def _():
        pivots = hop1[...] + hop3[...] + hop2[...]
        for y in range(NY):
            out[y] = pivots


def fan_pivots(own, hops):
    return pl.pallas_call(
        fan_pivots_kernel,
        out_shape=in_hbm((NY, NZ, CHUNK, FIRST)),
        in_specs=[VMEM] * 4,
        out_specs=VMEM,
        compiler_params=grant(8),
        name="fan_pivots",
    )(own, *hops)


def own_kernel(row_map, mask, ranks, near, u, v, out):
    row = lax.axis_index("row")
    col = lax.axis_index("col")
    t = pl.program_id(1)
    s = pl.program_id(0)
    tile = near[0, 0].astype(F32) * mask[s, t].astype(F32)
    out[0, 0] = tile + low_rank(kept_left(u[0, 0], ranks[s, t]), v[0, 0])

    @pl.when(row_map[2 * row + s] == t * 2 * NX + col)
    def _():
        out[0, 0] += SHIFT * eye()


def own_tiles(row_map, mask, ranks, near, u, v):
    def tiles(height):
        return pl.BlockSpec((1, 1, height, TILE), lambda s, t: (s, t, 0, 0))

    return pl.pallas_call(
        own_kernel,
        grid=(2, 2),
        out_shape=in_hbm((2, 2, TILE, TILE), F32),
        in_specs=[SMEM] * 3 + [tiles(TILE), tiles(KMAX), tiles(KMAX)],
        out_specs=tiles(TILE),
        compiler_params=grant(10),
        cost_estimate=pl.CostEstimate(flops=4 * 2 * TILE**3, bytes_accessed=7 << 20, transcendentals=0),
        name="own_tiles",
    )(row_map, mask, ranks, near, u, v)


def second_hop_kernel(cols, hop1, hop3, out):
    out[0] = cols[0] + hop1[...]
    out[1] = cols[1] + hop3[...]


def second_hop(cols, hops):
    return pl.pallas_call(
        second_hop_kernel,
        out_shape=jax.ShapeDtypeStruct((2, TILE, TILE), BF),
        in_specs=[VMEM] * 3,
        out_specs=VMEM,
        compiler_params=grant(8),
        name="second_hop",
    )(cols, *hops)


def panel_kernel(
    row_map, piv_own, piv_other, cols_own, cols_other, rows1, own, mult, lead_out, out,
    lead, piv, cols, rows, tiles, pivot_rows, out_buf, sems, out_sems,
):
    core = lax.axis_index("col") & 1
    row = lax.axis_index("row")
    moves = (
        (piv_own, piv.at[core]),
        (piv_other, piv.at[1 - core]),
        (cols_own, cols.at[core]),
        (cols_other, cols.at[1 - core]),
        (rows1, rows),
        (own.at[:, 1], tiles),
    )
    copies = [pltpu.make_async_copy(*move, sems.at[i]) for i, move in enumerate(moves)]
    for copy in copies:
        copy.start()
    copies[0].wait()
    copies[1].wait()

    def part(j, lanes):
        return piv[j, :, :, :, lanes].reshape(TILE, -1)

    firsts = slice(0, TILE)
    seconds = slice(TILE, 2 * TILE)
    factors = slice(2 * TILE, FIRST)
    inv0 = inverse(build(part(0, firsts), part(0, factors), True))
    row1 = part(1, firsts)
    mult_p1 = dot(part(0, seconds), inv0).astype(BF)
    lead[...] = mult_p1
    store = pltpu.make_async_copy(lead, lead_out, out_sems.at[2])
    store.start()
    inv1 = inverse(build(part(1, seconds), part(1, factors), True) - dot(mult_p1, row1))
    copies[2].wait()
    copies[3].wait()
    for s in range(2):
        held = row_map[2 * row + s]
        first = jnp.where(held > 0, dot(cols[0, s], inv0), 0.0).astype(BF)
        second = cols[1, s].astype(F32) - dot(first, row1)
        mult[s, :, :TILE] = first
        mult[s, :, TILE:] = jnp.where(held > 1, dot(second.astype(BF), inv1), 0.0).astype(BF)
    copies[4].wait()
    copies[5].wait()
    update(rows[..., :TILE].reshape(TILE, TILE), rows, lead, mult, tiles, pivot_rows, out, out_buf, out_sems, 1)
    store.wait()


def update(row0, rows, lead, mult, tiles, pivot_rows, out, out_buf, out_sems, t, ready=()):
    row1 = rows[..., TILE:].reshape(TILE, TILE).astype(F32) - dot(lead[...], row0)
    if t == 0:
        row1 = jnp.where(lax.axis_index("col") > 1, row1, 0.0)
    pivot_rows[:TILE] = row0
    pivot_rows[TILE:] = row1.astype(BF)
    for copy in ready:
        copy.wait()
    stores = []
    for s in range(2):
        out_buf[s] = (tiles[s] - dot(mult[s], pivot_rows[...])).astype(BF)
        stores.append(pltpu.make_async_copy(out_buf.at[s], out.at[s, t], out_sems.at[s]))
        stores[-1].start()
    for store in stores:
        store.wait()


def panel(row_map, piv_own, piv_other, cols_own, cols_other, rows1, own):
    return pl.pallas_call(
        panel_kernel,
        out_shape=(
            pltpu.VMEM((2, TILE, 2 * TILE), BF),
            in_hbm((TILE, TILE)),
            in_hbm((2, 2, TILE, TILE)),
        ),
        in_specs=[SMEM] + [ANY] * 6,
        out_specs=(VMEM, ANY, ANY),
        scratch_shapes=[
            pltpu.VMEM((TILE, TILE), BF),
            pltpu.VMEM((2, NY, NZ, CHUNK, FIRST), BF),
            pltpu.VMEM((2, 2, TILE, TILE), BF),
            pltpu.VMEM((NY, NZ, CHUNK, 2 * TILE), BF),
            pltpu.VMEM((2, TILE, TILE), F32),
            pltpu.VMEM((2 * TILE, TILE), BF),
            pltpu.VMEM((2, TILE, TILE), BF),
            pltpu.SemaphoreType.DMA((6,)),
            pltpu.SemaphoreType.DMA((3,)),
        ],
        compiler_params=grant(32),
        cost_estimate=pl.CostEstimate(flops=38 * 2 * TILE**3, bytes_accessed=5 << 20, transcendentals=0),
        name="panel",
    )(row_map, *pin(pltpu.HBM, piv_own, piv_other, cols_own, cols_other, rows1, own))


def last_kernel(rows, own, lead_in, mult, begun, out, lead, tiles, pivot_rows, out_buf, sems, out_sems):
    del begun
    col = lax.axis_index("col")
    copies = [
        pltpu.make_async_copy(lead_in, lead, sems.at[0]),
        pltpu.make_async_copy(own.at[:, 0], tiles, sems.at[1]),
    ]
    for copy in copies:
        copy.start()
    row0 = rows[..., :TILE].reshape(TILE, TILE).astype(F32)
    row0 = jnp.where(col > 0, row0, 0.0).astype(BF)
    copies[0].wait()
    update(row0, rows, lead, mult, tiles, pivot_rows, out, out_buf, out_sems, 0, copies[1:])


def last(rows0, own, lead, mult, begun):
    return pl.pallas_call(
        last_kernel,
        out_shape=in_hbm((2, 2, TILE, TILE)),
        in_specs=[VMEM, ANY, ANY, VMEM, ANY],
        out_specs=ANY,
        input_output_aliases={4: 0},
        scratch_shapes=[
            pltpu.VMEM((TILE, TILE), BF),
            pltpu.VMEM((2, TILE, TILE), F32),
            pltpu.VMEM((2 * TILE, TILE), BF),
            pltpu.VMEM((2, TILE, TILE), BF),
            pltpu.SemaphoreType.DMA((2,)),
            pltpu.SemaphoreType.DMA((2,)),
        ],
        compiler_params=grant(28),
        cost_estimate=pl.CostEstimate(flops=6 * 2 * TILE**3, bytes_accessed=6 << 20, transcendentals=0),
        name="last",
    )(*pin(pltpu.VMEM, rows0), *pin(pltpu.HBM, own, lead), *pin(pltpu.VMEM, mult), *pin(pltpu.HBM, begun))


def pairs(source, target):
    return [(source * 2 + core, target * 2 + core) for core in range(2)]


def body(near_tiles, basis_u, basis_v, near_mask, ranks, row_map):
    near = near_tiles.reshape(2, 2, TILE, TILE)
    u = basis_u.reshape(2, 2, KMAX, TILE)
    v = basis_v.reshape(2, 2, KMAX, TILE)
    mask = near_mask.reshape(2, 2)
    ranks = ranks.reshape(2, 2)
    x = lax.axis_index("col") >> 1

    send = head(False, row_map, mask, ranks, near, u, v)

    def scatter(part):
        return lax.all_to_all(part, "row", 0, 0)

    def beside():
        cols = columns(row_map, mask, ranks, near, u, v)
        hop = [lax.ppermute(cols, "col", pairs(0, to)) for to in (1, 3)]
        return cols, hop, own_tiles(row_map, mask, ranks, near, u, v)

    def apart():
        again = head(True, row_map, mask, ranks, near, u, v)
        got = [scatter(send), scatter(again)]
        return take(row_map, *got), beside()

    def merged():
        got = scatter(send)
        return take(row_map, got, got), beside()

    device = jnp.arange(NROWS, dtype=jnp.int32) >> 1
    apart_by = jnp.sum(jnp.where(row_map == 0, device, 0) - jnp.where(row_map == 1, device, 0))
    one_device = apart_by == 0
    line, (cols, hop, own) = lax.cond(one_device, apart, merged)

    z_groups = [[y * NZ + z for z in range(NZ)] for y in range(NY)]
    y_groups = [[y * NZ + z for y in range(NY)] for z in range(NZ)]
    line = lax.all_to_all(line, "row", 0, 0, axis_index_groups=z_groups)

    def gather(part):
        return lax.all_to_all(part, "row", 0, 0, axis_index_groups=y_groups)

    pivots, rows0, rows1 = fan(line)
    rows1 = gather(rows1)
    hops = [lax.ppermute(pivots, "col", pairs(0, to)) for to in (1, 3, 2)]
    cols = jnp.where(x == 0, cols, hop[0] + hop[1])
    hops, rows1, cols = lax.optimization_barrier((hops, rows1, cols))
    hop = [lax.ppermute(cols[s], "col", pairs(source, 2)) for s, source in enumerate((1, 3))]
    piv = gather(fan_pivots(pivots, hops))
    cols = second_hop(cols, hop)
    swap = [(c, c ^ 1) for c in range(2 * NX)]
    rows0, piv, cols = lax.optimization_barrier((rows0, piv, cols))
    rows0 = gather(rows0)
    piv_other = lax.ppermute(piv, "col", swap)
    cols_other = lax.ppermute(cols, "col", swap)
    mult, lead, begun = panel(row_map, piv, piv_other, cols, cols_other, rows1, own)
    out = last(rows0, own, lead, mult, begun)
    return out.reshape(2, 2, 1, TILE, TILE)


def solution(mesh):
    return jax.shard_map(
        body,
        mesh=mesh,
        in_specs=(
            P("row", None, "col", None, None),
            P("row", None, "col", None, None),
            P("row", None, "col", None, None),
            P("row", None, "col"),
            P("row", None, "col"),
            P(),
        ),
        out_specs=P("row", None, "col", None, None),
        check_vma=False,
    )
```

```python
import math

import jax
import jax.numpy as jnp
from jax import lax
from jax.experimental import pallas as pl
from jax.experimental.pallas import tpu as pltpu
from jax.sharding import PartitionSpec as P

TILE = 512
KMAX = 64
LANES = 128
WIDE = TILE + LANES
FIRST = TILE + WIDE
BLOCKS = TILE // LANES
CHUNK = 16
PARTS = TILE // CHUNK
NROWS = 64
SHIFT = 1.1 * math.sqrt(TILE)
NY, NZ, NX = 4, 8, 4
BF = jnp.bfloat16
F32 = jnp.float32

SMEM = pl.BlockSpec(memory_space=pltpu.SMEM)
VMEM = pl.BlockSpec(memory_space=pltpu.VMEM)
ANY = pl.BlockSpec(memory_space=pl.ANY)


def grant(mib):
    return pltpu.CompilerParams(vmem_limit_bytes=mib << 20)


def in_hbm(shape, dtype=BF):
    return pltpu.HBM(shape, dtype)


def pin(space, *arrays):
    return [pltpu.with_memory_space_constraint(array, space) for array in arrays]


def dot(a, b):
    return jnp.dot(a, b, preferred_element_type=F32)


def split(a):
    high = a.astype(BF)
    return high, (a - high.astype(F32)).astype(BF)


def dot_hi(a, b):
    left = jnp.concatenate([a[0], a[0], a[1]], axis=1)
    return dot(left, jnp.concatenate([b[0], b[1], b[0]], axis=0))


def eye():
    rows = lax.broadcasted_iota(jnp.int32, (TILE, TILE), 0)
    cols = lax.broadcasted_iota(jnp.int32, (TILE, TILE), 1)
    return (rows == cols).astype(F32)


def low_rank(left, right):
    return lax.dot_general(left, right, (((0,), (0,)), ((), ())), preferred_element_type=F32)


def build(near, factors, diag):
    factors = factors.reshape(BLOCKS, 2, KMAX, LANES)
    left = jnp.concatenate([factors[k, 0] for k in range(BLOCKS)], axis=1)
    right = jnp.concatenate([factors[k, 1] for k in range(BLOCKS)], axis=1)
    tile = near.astype(F32) + low_rank(left, right)
    return tile + jnp.where(diag, SHIFT, 0.0) * eye()


def inverse(pivot):
    ident = eye()
    e = ident - pivot * (1.0 / SHIFT)
    es = split(e)
    e2 = dot_hi(es, es)
    e2s = split(e2)
    total = split(ident + e + e2 + dot_hi(es, e2s))
    e4 = dot_hi(e2s, e2s)
    whole = total[0].astype(F32) + total[1].astype(F32) + dot_hi(total, split(e4))
    return (whole * (1.0 / SHIFT)).astype(BF)


def kept_left(u, rank):
    rows = lax.broadcasted_iota(jnp.int32, (KMAX, TILE), 0)
    return jnp.where(rows < rank, u.astype(F32), 0.0).astype(BF)


def lane_blocks(left, right):
    parts = []
    for k in range(BLOCKS):
        cut = slice(k * LANES, (k + 1) * LANES)
        parts += [left[:, cut], right[:, cut]]
    return jnp.concatenate(parts, axis=0)


def find_owners(row_map):
    def step(slot, found):
        held = row_map[slot]
        return jnp.where(held == 0, slot, found[0]), jnp.where(held == 1, slot, found[1])

    return lax.fori_loop(0, NROWS, step, (0, 0), unroll=8)


def head_kernel(second, row_map, mask, ranks, near, u, v, out, send, near_buf, u_buf, v_buf, sems, out_sems):
    row = lax.axis_index("row")
    col = lax.axis_index("col")
    owners = find_owners(row_map)
    panel = 1 if second else jnp.where(row == owners[0] >> 1, 0, 1)
    s = jnp.where(panel == 0, owners[0], owners[1]) & 1
    moves = [(u.at[s], u_buf), (v.at[s], v_buf)]
    moves += [(near.at[s, t], near_buf.at[t]) for t in (1, 0)]
    copies = [pltpu.make_async_copy(*move, sems.at[i]) for i, move in enumerate(moves)]
    for copy in copies:
        copy.start()
    copies[0].wait()
    copies[1].wait()
    stores = []
    for t in (1, 0):
        low = low_rank(kept_left(u_buf[t], ranks[s, t]), v_buf[t])
        copies[3 - t].wait()
        tile = (near_buf[t].astype(F32) * mask[s, t].astype(F32) + low).astype(BF)
        lanes = pl.ds(t * WIDE, WIDE if t == 0 else TILE)
        send[:, :, t * WIDE : t * WIDE + TILE] = tile.reshape(PARTS, CHUNK, TILE)
        if t == 0:

            @pl.when(col == panel)
            def _():
                raw = near_buf[0] * mask[s, 0].astype(F32).astype(BF)
                factors = lane_blocks(kept_left(u_buf[0], ranks[s, 0]), v_buf[0])
                send[:, :, :TILE] = raw.reshape(PARTS, CHUNK, TILE)
                send[:, :, TILE:WIDE] = factors.reshape(PARTS, CHUNK, LANES)

        stores.append(pltpu.make_async_copy(send.at[:, :, lanes], out.at[:, :, lanes], out_sems.at[t]))
        stores[-1].start()
    for store in stores:
        store.wait()


def head(second, row_map, mask, ranks, near, u, v):
    def kernel(*refs):
        head_kernel(second, *refs)

    return pl.pallas_call(
        kernel,
        out_shape=in_hbm((PARTS, CHUNK, WIDE + TILE)),
        in_specs=[SMEM] * 3 + [ANY] * 3,
        out_specs=ANY,
        scratch_shapes=[
            pltpu.VMEM((PARTS, CHUNK, WIDE + TILE), BF),
            pltpu.VMEM((2, TILE, TILE), BF),
            pltpu.VMEM((2, KMAX, TILE), BF),
            pltpu.VMEM((2, KMAX, TILE), BF),
            pltpu.SemaphoreType.DMA((4,)),
            pltpu.SemaphoreType.DMA((2,)),
        ],
        compiler_params=grant(12),
        name="head_again" if second else "head",
    )(row_map, mask, ranks, near, u, v)


def columns_kernel(row_map, mask, ranks, near, u, v, cols):
    row = lax.axis_index("row")
    col = lax.axis_index("col")
    for s in range(2):
        tile = near[s, 0].astype(F32) * mask[s, 0].astype(F32)
        tile = tile + low_rank(kept_left(u[s, 0], ranks[s, 0]), v[s, 0])
        tile = tile + jnp.where(row_map[2 * row + s] == col, SHIFT, 0.0) * eye()
        cols[s] = tile.astype(BF)


def columns(row_map, mask, ranks, near, u, v):
    def tiles(height):
        return pl.BlockSpec((2, 1, height, TILE), lambda i: (0, 0, 0, 0))

    return pl.pallas_call(
        columns_kernel,
        grid=(1,),
        out_shape=in_hbm((2, TILE, TILE)),
        in_specs=[SMEM] * 3 + [tiles(TILE), tiles(KMAX), tiles(KMAX)],
        out_specs=pl.BlockSpec((2, TILE, TILE), lambda i: (0, 0, 0)),
        compiler_params=grant(10),
        name="columns",
    )(row_map, mask, ranks, near, u, v)


def take_kernel(row_map, got0, got1, out, chunk, sems):
    copies = []
    for k, (got, owner) in enumerate(zip((got0, got1), find_owners(row_map))):
        copies.append(pltpu.make_async_copy(got.at[owner >> 1], chunk.at[k], sems.at[k]))
        copies[-1].start()
    for copy in copies:
        copy.wait()
    core = lax.axis_index("col") & 1
    parts = [chunk[0, :, :TILE], chunk[1, :, :TILE], chunk[core, :, TILE:WIDE]]
    parts += [chunk[0, :, WIDE:], chunk[1, :, WIDE:]]
    whole = jnp.concatenate(parts, axis=1)
    for z in range(NZ):
        out[z] = whole


def take(row_map, got0, got1):
    return pl.pallas_call(
        take_kernel,
        out_shape=in_hbm((NZ, CHUNK, FIRST + 2 * TILE)),
        in_specs=[SMEM, ANY, ANY],
        out_specs=VMEM,
        scratch_shapes=[pltpu.VMEM((2, CHUNK, WIDE + TILE), BF), pltpu.SemaphoreType.DMA((2,))],
        compiler_params=grant(8),
        name="take",
    )(row_map, got0, got1)


def fan_kernel(line, pivots, rows0, rows1):
    pivots[...] = line[:, :, :FIRST]
    for y in range(NY):
        rows0[y] = line[:, :, : 2 * TILE]
        rows1[y] = line[:, :, FIRST:]


def fan(line):
    rows = in_hbm((NY, NZ, CHUNK, 2 * TILE))
    return pl.pallas_call(
        fan_kernel,
        out_shape=(jax.ShapeDtypeStruct((NZ, CHUNK, FIRST), BF), rows, rows),
        in_specs=[VMEM],
        out_specs=(VMEM,) * 3,
        compiler_params=grant(8),
        name="fan",
    )(line)


def fan_pivots_kernel(own, hop1, hop3, hop2, out):
    x = lax.axis_index("col") >> 1

    @pl.when(x == 0)
    def _():
        for y in range(NY):
            out[y] = own[...]

    @pl.when(x != 0)
    def _():
        pivots = hop1[...] + hop3[...] + hop2[...]
        for y in range(NY):
            out[y] = pivots


def fan_pivots(own, hops):
    return pl.pallas_call(
        fan_pivots_kernel,
        out_shape=in_hbm((NY, NZ, CHUNK, FIRST)),
        in_specs=[VMEM] * 4,
        out_specs=VMEM,
        compiler_params=grant(8),
        name="fan_pivots",
    )(own, *hops)


def own_kernel(row_map, mask, ranks, near, u, v, out):
    row = lax.axis_index("row")
    col = lax.axis_index("col")
    t = pl.program_id(1)
    s = pl.program_id(0)
    tile = near[0, 0].astype(F32) * mask[s, t].astype(F32)
    out[0, 0] = tile + low_rank(kept_left(u[0, 0], ranks[s, t]), v[0, 0])

    @pl.when(row_map[2 * row + s] == t * 2 * NX + col)
    def _():
        out[0, 0] += SHIFT * eye()


def own_tiles(row_map, mask, ranks, near, u, v):
    def tiles(height):
        return pl.BlockSpec((1, 1, height, TILE), lambda s, t: (s, t, 0, 0))

    return pl.pallas_call(
        own_kernel,
        grid=(2, 2),
        out_shape=in_hbm((2, 2, TILE, TILE), F32),
        in_specs=[SMEM] * 3 + [tiles(TILE), tiles(KMAX), tiles(KMAX)],
        out_specs=tiles(TILE),
        compiler_params=grant(10),
        cost_estimate=pl.CostEstimate(flops=4 * 2 * TILE**3, bytes_accessed=7 << 20, transcendentals=0),
        name="own_tiles",
    )(row_map, mask, ranks, near, u, v)


def second_hop_kernel(cols, hop1, hop3, out):
    out[0] = cols[0] + hop1[...]
    out[1] = cols[1] + hop3[...]


def second_hop(cols, hops):
    return pl.pallas_call(
        second_hop_kernel,
        out_shape=jax.ShapeDtypeStruct((2, TILE, TILE), BF),
        in_specs=[VMEM] * 3,
        out_specs=VMEM,
        compiler_params=grant(8),
        name="second_hop",
    )(cols, *hops)


def panel_kernel(
    row_map, piv_own, piv_other, cols_own, cols_other, rows1, own, mult, lead_out, out,
    lead, piv, cols, rows, tiles, pivot_rows, out_buf, sems, out_sems,
):
    core = lax.axis_index("col") & 1
    row = lax.axis_index("row")
    moves = (
        (piv_own, piv.at[core]),
        (piv_other, piv.at[1 - core]),
        (cols_own, cols.at[core]),
        (cols_other, cols.at[1 - core]),
        (rows1, rows),
        (own.at[:, 1], tiles),
    )
    copies = [pltpu.make_async_copy(*move, sems.at[i]) for i, move in enumerate(moves)]
    for copy in copies:
        copy.start()
    copies[0].wait()
    copies[1].wait()

    def part(j, lanes):
        return piv[j, :, :, :, lanes].reshape(TILE, -1)

    firsts = slice(0, TILE)
    seconds = slice(TILE, 2 * TILE)
    factors = slice(2 * TILE, FIRST)
    inv0 = inverse(build(part(0, firsts), part(0, factors), True))
    row1 = part(1, firsts)
    mult_p1 = dot(part(0, seconds), inv0).astype(BF)
    lead[...] = mult_p1
    store = pltpu.make_async_copy(lead, lead_out, out_sems.at[2])
    store.start()
    inv1 = inverse(build(part(1, seconds), part(1, factors), True) - dot(mult_p1, row1))
    copies[2].wait()
    copies[3].wait()
    for s in range(2):
        held = row_map[2 * row + s]
        first = jnp.where(held > 0, dot(cols[0, s], inv0), 0.0).astype(BF)
        second = cols[1, s].astype(F32) - dot(first, row1)
        mult[s, :, :TILE] = first
        mult[s, :, TILE:] = jnp.where(held > 1, dot(second.astype(BF), inv1), 0.0).astype(BF)
    copies[4].wait()
    copies[5].wait()
    update(rows[..., :TILE].reshape(TILE, TILE), rows, lead, mult, tiles, pivot_rows, out, out_buf, out_sems, 1)
    store.wait()


def update(row0, rows, lead, mult, tiles, pivot_rows, out, out_buf, out_sems, t, ready=()):
    row1 = rows[..., TILE:].reshape(TILE, TILE).astype(F32) - dot(lead[...], row0)
    if t == 0:
        row1 = jnp.where(lax.axis_index("col") > 1, row1, 0.0)
    pivot_rows[:TILE] = row0
    pivot_rows[TILE:] = row1.astype(BF)
    stores = []
    for s in range(2):
        if ready:
            ready[s].wait()
        out_buf[s] = (tiles[s] - dot(mult[s], pivot_rows[...])).astype(BF)
        stores.append(pltpu.make_async_copy(out_buf.at[s], out.at[s, t], out_sems.at[s]))
        stores[-1].start()
    for store in stores:
        store.wait()


def panel(row_map, piv_own, piv_other, cols_own, cols_other, rows1, own):
    return pl.pallas_call(
        panel_kernel,
        out_shape=(
            pltpu.VMEM((2, TILE, 2 * TILE), BF),
            in_hbm((TILE, TILE)),
            in_hbm((2, 2, TILE, TILE)),
        ),
        in_specs=[SMEM] + [ANY] * 6,
        out_specs=(VMEM, ANY, ANY),
        scratch_shapes=[
            pltpu.VMEM((TILE, TILE), BF),
            pltpu.VMEM((2, NY, NZ, CHUNK, FIRST), BF),
            pltpu.VMEM((2, 2, TILE, TILE), BF),
            pltpu.VMEM((NY, NZ, CHUNK, 2 * TILE), BF),
            pltpu.VMEM((2, TILE, TILE), F32),
            pltpu.VMEM((2 * TILE, TILE), BF),
            pltpu.VMEM((2, TILE, TILE), BF),
            pltpu.SemaphoreType.DMA((6,)),
            pltpu.SemaphoreType.DMA((3,)),
        ],
        compiler_params=grant(32),
        cost_estimate=pl.CostEstimate(flops=38 * 2 * TILE**3, bytes_accessed=5 << 20, transcendentals=0),
        name="panel",
    )(row_map, *pin(pltpu.HBM, piv_own, piv_other, cols_own, cols_other, rows1, own))


def last_kernel(rows, own, lead_in, mult, begun, out, lead, tiles, pivot_rows, out_buf, sems, out_sems):
    del begun
    col = lax.axis_index("col")
    copies = [
        pltpu.make_async_copy(lead_in, lead, sems.at[0]),
        pltpu.make_async_copy(own.at[0, 0], tiles.at[0], sems.at[1]),
        pltpu.make_async_copy(own.at[1, 0], tiles.at[1], sems.at[2]),
    ]
    for copy in copies:
        copy.start()
    row0 = rows[..., :TILE].reshape(TILE, TILE).astype(F32)
    row0 = jnp.where(col > 0, row0, 0.0).astype(BF)
    copies[0].wait()
    update(row0, rows, lead, mult, tiles, pivot_rows, out, out_buf, out_sems, 0, copies[1:])


def last(rows0, own, lead, mult, begun):
    return pl.pallas_call(
        last_kernel,
        out_shape=in_hbm((2, 2, TILE, TILE)),
        in_specs=[VMEM, ANY, ANY, VMEM, ANY],
        out_specs=ANY,
        input_output_aliases={4: 0},
        scratch_shapes=[
            pltpu.VMEM((TILE, TILE), BF),
            pltpu.VMEM((2, TILE, TILE), F32),
            pltpu.VMEM((2 * TILE, TILE), BF),
            pltpu.VMEM((2, TILE, TILE), BF),
            pltpu.SemaphoreType.DMA((3,)),
            pltpu.SemaphoreType.DMA((2,)),
        ],
        compiler_params=grant(28),
        cost_estimate=pl.CostEstimate(flops=6 * 2 * TILE**3, bytes_accessed=6 << 20, transcendentals=0),
        name="last",
    )(*pin(pltpu.VMEM, rows0), *pin(pltpu.HBM, own, lead), *pin(pltpu.VMEM, mult), *pin(pltpu.HBM, begun))


def pairs(source, target):
    return [(source * 2 + core, target * 2 + core) for core in range(2)]


def body(near_tiles, basis_u, basis_v, near_mask, ranks, row_map):
    near = near_tiles.reshape(2, 2, TILE, TILE)
    u = basis_u.reshape(2, 2, KMAX, TILE)
    v = basis_v.reshape(2, 2, KMAX, TILE)
    mask = near_mask.reshape(2, 2)
    ranks = ranks.reshape(2, 2)
    x = lax.axis_index("col") >> 1

    send = head(False, row_map, mask, ranks, near, u, v)

    def scatter(part):
        return lax.all_to_all(part, "row", 0, 0)

    cols = columns(row_map, mask, ranks, near, u, v)
    hop = [lax.ppermute(cols, "col", pairs(0, to)) for to in (1, 3)]
    own = own_tiles(row_map, mask, ranks, near, u, v)
    device = jnp.arange(NROWS, dtype=jnp.int32) >> 1
    apart_by = jnp.sum(jnp.where(row_map == 0, device, 0) - jnp.where(row_map == 1, device, 0))
    got, hop, own, apart_by = lax.optimization_barrier((scatter(send), hop, own, apart_by))

    def apart():
        again = head(True, row_map, mask, ranks, near, u, v)
        return take(row_map, got, scatter(again))

    def merged():
        return take(row_map, got, got)

    line = lax.cond(apart_by == 0, apart, merged)

    z_groups = [[y * NZ + z for z in range(NZ)] for y in range(NY)]
    y_groups = [[y * NZ + z for y in range(NY)] for z in range(NZ)]
    line = lax.all_to_all(line, "row", 0, 0, axis_index_groups=z_groups)

    def gather(part):
        return lax.all_to_all(part, "row", 0, 0, axis_index_groups=y_groups)

    pivots, rows0, rows1 = fan(line)
    rows1 = gather(rows1)
    hops = [lax.ppermute(pivots, "col", pairs(0, to)) for to in (3, 1, 2)]
    cols = jnp.where(x == 0, cols, hop[0] + hop[1])
    hops, rows1, cols = lax.optimization_barrier((hops, rows1, cols))
    hop = [lax.ppermute(cols[s], "col", pairs(source, 2)) for s, source in enumerate((1, 3))]
    piv = gather(fan_pivots(pivots, hops))
    cols = second_hop(cols, hop)
    swap = [(c, c ^ 1) for c in range(2 * NX)]
    rows0, piv, cols = lax.optimization_barrier((rows0, piv, cols))
    rows0 = gather(rows0)
    piv_other = lax.ppermute(piv, "col", swap)
    cols_other = lax.ppermute(cols, "col", swap)
    mult, lead, begun = panel(row_map, piv, piv_other, cols, cols_other, rows1, own)
    out = last(rows0, own, lead, mult, begun)
    return out.reshape(2, 2, 1, TILE, TILE)


def solution(mesh):
    return jax.shard_map(
        body,
        mesh=mesh,
        in_specs=(
            P("row", None, "col", None, None),
            P("row", None, "col", None, None),
            P("row", None, "col", None, None),
            P("row", None, "col"),
            P("row", None, "col"),
            P(),
        ),
        out_specs=P("row", None, "col", None, None),
        check_vma=False,
    )
```
